512 devices in a mesh: seq: 128 (over x, y, z_hi, core), ch: 4 (over z_lo).
Axes of the slice: x: 4, y: 4, z: 16 (z_hi: 4, z_lo: 4; z = z_hi * 4 + z_lo), core: 2. Of those that a mesh axis runs over, the one named last changes fastest.
Arguments:
- signal_branch: bfloat16 [64, 65536], P('ch', 'seq'), may hold values from -6 to 6
- leading_multiplier: bfloat16 [64, 65536], P('ch', 'seq'), may hold values from -6 to 6
- trailing_multiplier: bfloat16 [64, 65536], P('ch', 'seq'), may hold values from -6 to 6
- loss_upstream_adjoint: bfloat16 [64, 65536], P('ch', 'seq'), may hold values from -6 to 6
- kernel_net_hidden: bfloat16 [64, 65536], P('ch', 'seq'), may hold values from -6 to 6
- kernel_readout_matrix: float32 [2, 64, 64], P(None, 'ch'), may hold values from -0.75 to 0.75
- kernel_attenuation: float32 [2, 64], P(None, 'ch'), may hold values from 7.6293945e-06 to 0.033333335
Outputs:
- signal_branch_adjoint: bfloat16 [64, 65536], P('ch', 'seq')
- leading_multiplier_adjoint: bfloat16 [64, 65536], P('ch', 'seq')
- trailing_multiplier_adjoint: bfloat16 [64, 65536], P('ch', 'seq')
- readout_adjoint_factored: bfloat16 [2, 64, 64], P(None, 'ch')
- hidden_adjoint_factored: bfloat16 [64, 65536], P('ch', 'seq')
The draws below stay inside these ranges and needn't reach their ends.
All inputs are finite; a program needn't handle non-finite values.
Results may differ from the reference program's by a relative error of at most 0.003.
Values may be sent and summed in bfloat16 or wider, within the bound.
A program may use at most 64 MiB of HBM per device.

```python
import math
import jax
import jax.numpy as jnp
from jax import lax

KERNEL_WIDTHS = 64
FEATURES = 64
GENOME_SPAN = 65536


def levels(key, extent, pieces, smallest, high):
    loudness = 1.0
    for dim, shards_of in pieces:
        steps = jax.random.uniform(jax.random.fold_in(jax.random.fold_in(key, 6), dim), (shards_of,), jnp.float32, smallest / len(pieces), high / len(pieces))
        loudness = loudness * jnp.repeat(jnp.exp(steps), extent[dim] // shards_of).reshape((-1,) + (1,) * (len(extent) - 1 - dim))
    return loudness


def scatter_about(own_key, dims, deviation, reach, split=(), held_as=jnp.bfloat16):
    entries = deviation * jax.random.normal(own_key, dims, jnp.float32)
    if split:
        entries = entries * levels(own_key, dims, split, -0.22, 0.18)
    return jnp.clip(entries, -reach, reach).astype(held_as)


def setup_inputs(seed: int = 0) -> dict:
    keys = jax.random.split(jax.random.key(seed), 8)
    signal_branch = scatter_about(keys[0], (KERNEL_WIDTHS, GENOME_SPAN), 1.0, 6.0, ((0, 4), (1, 128)))
    leading_multiplier = scatter_about(keys[1], (KERNEL_WIDTHS, GENOME_SPAN), 1.0, 6.0, ((0, 4), (1, 128)))
    trailing_multiplier = scatter_about(keys[2], (KERNEL_WIDTHS, GENOME_SPAN), 1.0, 6.0, ((0, 4), (1, 128)))
    loss_upstream_adjoint = scatter_about(keys[3], (KERNEL_WIDTHS, GENOME_SPAN), 1.0, 6.0, ((0, 4), (1, 128)))
    kernel_net_hidden = scatter_about(keys[4], (FEATURES, GENOME_SPAN), 1.0, 6.0, ((0, 4), (1, 128)))
    kernel_readout_matrix = scatter_about(keys[5], (2, KERNEL_WIDTHS, FEATURES), FEATURES ** -0.5, 0.75, ((1, 4),), jnp.float32)
    kernel_attenuation = jnp.clip(jnp.exp(math.log(0.033333335) - 8.382305 * jax.random.uniform(keys[6], (2, KERNEL_WIDTHS), jnp.float32) ** levels(keys[6], (2, KERNEL_WIDTHS), ((1, 4),), -0.2, 0.2)), 7.62939453125e-06, 0.033333335)
    return dict(signal_branch=signal_branch, leading_multiplier=leading_multiplier, trailing_multiplier=trailing_multiplier, loss_upstream_adjoint=loss_upstream_adjoint, kernel_net_hidden=kernel_net_hidden, kernel_readout_matrix=kernel_readout_matrix, kernel_attenuation=kernel_attenuation)


def reference(signal_branch, leading_multiplier, trailing_multiplier, loss_upstream_adjoint, kernel_net_hidden, kernel_readout_matrix, kernel_attenuation):
    highest = lax.Precision.HIGHEST
    genome_extent = signal_branch.shape[1]
    total = 2 * genome_extent
    position = jnp.arange(genome_extent).astype(jnp.float32)
    window = jnp.exp(-kernel_attenuation[:, :, None] * position)
    scale = jnp.sqrt(jnp.expm1(-2.0 * kernel_attenuation) / jnp.expm1(-2.0 * kernel_attenuation * genome_extent))
    feat_full = kernel_net_hidden.astype(jnp.float32)
    base = jnp.einsum('ocf,fl->ocl', kernel_readout_matrix, feat_full, precision=highest)
    filt = base * window * scale[:, :, None]

    def spectrum(signal):
        return jnp.fft.rfft(signal, n=total, axis=-1)

    def inverse(spec):
        return jnp.fft.irfft(spec, n=total, axis=-1)[..., :genome_extent]
    branch_source = signal_branch.astype(jnp.float32)
    gate_a = leading_multiplier.astype(jnp.float32)
    gate_b = trailing_multiplier.astype(jnp.float32)
    grad_y = loss_upstream_adjoint.astype(jnp.float32)
    spec_v = spectrum(branch_source)
    spec_h1 = spectrum(filt[0])
    spec_h2 = spectrum(filt[1])
    first_u = inverse(spec_v * spec_h1)
    second_z = gate_a * first_u
    spec_z = spectrum(second_z)
    second_u = inverse(spec_z * spec_h2)
    grad_two = grad_y * gate_b
    spec_g2 = spectrum(grad_two)
    grad_z = inverse(spec_g2 * jnp.conj(spec_h2))
    grad_h2 = inverse(spec_g2 * jnp.conj(spec_z))
    grad_one = grad_z * gate_a
    spec_g1 = spectrum(grad_one)
    branch_adjoint = inverse(spec_g1 * jnp.conj(spec_h1))
    grad_h1 = inverse(spec_g1 * jnp.conj(spec_v))
    signal_branch_adjoint = branch_adjoint.astype(jnp.bfloat16)
    leading_multiplier_adjoint = (grad_z * first_u).astype(jnp.bfloat16)
    trailing_multiplier_adjoint = (grad_y * second_u).astype(jnp.bfloat16)
    dhw = jnp.stack([grad_h1, grad_h2]) * window * scale[:, :, None] / math.sqrt(genome_extent)
    readout_adjoint_factored = jnp.einsum('ocl,fl->ocf', dhw, feat_full, precision=highest).astype(jnp.bfloat16)
    hidden_adjoint_factored = jnp.einsum('ocf,ocl->fl', kernel_readout_matrix, dhw, precision=highest).astype(jnp.bfloat16)
    return (signal_branch_adjoint, leading_multiplier_adjoint, trailing_multiplier_adjoint, readout_adjoint_factored, hidden_adjoint_factored)
```

```python
import math

import jax
import jax.numpy as jnp
import ml_dtypes
import numpy as np
from jax import lax
from jax.experimental import pallas as pl
from jax.experimental.pallas import tpu as pltpu
from jax.sharding import PartitionSpec as P

F32 = jnp.float32
BF16 = jnp.bfloat16
SEQ = 128
CH = 4
WIDTH = 16
LOCUS = 512
MESH = pl.DeviceIdType.MESH


def owner_of(channel, group):
    high = lax.rem(lax.div(channel, 4) + lax.rem(channel, 4) + group, 4)
    return channel * 8 + 2 * high


def halves(value):
    high = value.astype(BF16)
    return high, (value - high.astype(F32)).astype(BF16)


def np_halves(value):
    value = value.astype(np.float32)
    high = value.astype(ml_dtypes.bfloat16)
    return high, (value - high.astype(np.float32)).astype(ml_dtypes.bfloat16)


def make_tables():
    length = SEQ * LOCUS
    points = 2 * length
    order = np.concatenate([2 * np.arange(128), 2 * np.arange(128) + 1])
    coarse = np.arange(256) + 0.5
    angle = 2.0 * np.pi * coarse[:, None] * order[None, :] / 512.0
    first = np.concatenate([np.cos(angle), -np.sin(angle)], 0)
    first_hi, first_lo = np_halves(first)
    w1 = np.concatenate([first_hi, first_hi, first_lo], 1)
    last_hi, last_lo = np_halves(first.T / length)
    w1t = np.concatenate([last_hi, last_hi, last_lo], 1)
    fine = np.arange(256)
    angle = 2.0 * np.pi * (fine[:, None] * fine[None, :] % 256) / 256.0
    cos, sin = np.cos(angle), np.sin(angle)
    mid_hi, mid_lo = np_halves(np.block([[cos, -sin], [sin, cos]]))
    w2 = np.concatenate([mid_hi, mid_hi, mid_lo], 0)
    back_hi, back_lo = np_halves(np.block([[cos, sin], [-sin, cos]]))
    w2c = np.concatenate([back_hi, back_hi, back_lo], 0)
    angle = 2.0 * np.pi * coarse[:, None] * fine[None, :] / points
    return w1, w1t, w2, w2c, np.cos(angle).astype(np.float32), -np.sin(angle).astype(np.float32)


def tile_rows(index, count):
    return pl.ds(pl.multiple_of(index * count, count), count)


def send(src, dst, send_sem, recv_sem, seq, ch):
    pltpu.make_async_remote_copy(
        src_ref=src,
        dst_ref=dst,
        send_sem=send_sem,
        recv_sem=recv_sem,
        device_id=(seq, ch),
        device_id_type=MESH,
    ).start()


def drain(ref, sem):
    pltpu.make_async_copy(ref, ref, sem).wait()


def greet(barrier, seq, ch):
    pl.semaphore_signal(barrier, inc=1, device_id=(seq, ch), device_id_type=MESH)


def inbound_kernel(
    msgb,
    hidden,
    readout,
    windows,
    inb,
    inh,
    feat,
    hbuf,
    f_send,
    f_recv,
    b_send,
    b_recv,
    h_send,
    h_recv,
):
    seq = lax.axis_index("seq")
    ch = lax.axis_index("ch")
    channel = lax.div(seq, 8)
    is_owner = owner_of(channel, ch) == seq
    barrier = pltpu.get_barrier_semaphore()
    for step in range(1, CH):
        greet(barrier, seq, lax.rem(ch + step, CH))

    @pl.when(is_owner)
    def _():
        @pl.loop(1, SEQ)
        def _(step):
            greet(barrier, lax.rem(seq + step, SEQ), ch)

        pl.semaphore_wait(barrier, WIDTH - 1 + CH - 1)

    @pl.when(jnp.logical_not(is_owner))
    def _():
        pl.semaphore_wait(barrier, WIDTH + CH - 1)

    mine = tile_rows(ch, WIDTH)
    for step in range(1, CH):
        send(hidden, feat.at[mine], f_send, f_recv, seq, lax.rem(ch + step, CH))
    feat[mine, :] = hidden[...]

    def spread(source, target, rows, send_sem, recv_sem):
        slot = tile_rows(seq, rows)

        @pl.loop(0, WIDTH)
        def _(step):
            to = lax.rem(channel + step, WIDTH)
            owner = owner_of(to, ch)
            piece = source.at[tile_rows(to, rows)]

            @pl.when(owner != seq)
            def _():
                send(piece, target.at[slot], send_sem, recv_sem, owner, ch)

            @pl.when(owner == seq)
            def _():
                pltpu.make_async_copy(piece, target.at[slot], recv_sem).start()

    spread(msgb, inb, 16, b_send, b_recv)
    drain(feat.at[pl.ds(0, 3 * WIDTH)], f_recv)
    filt = (
        jnp.dot(
            readout[...],
            feat[...].astype(F32),
            precision=lax.Precision.HIGHEST,
            preferred_element_type=F32,
        )
        * windows[...]
    )
    for order in range(2):
        for part in range(4):
            hbuf[pl.ds(order * 4 + part, WIDTH, stride=8), :] = filt[
                order * WIDTH : (order + 1) * WIDTH, part * 128 : (part + 1) * 128
            ]
    spread(hbuf, inh, 8, h_send, h_recv)
    drain(feat.at[pl.ds(0, 3 * WIDTH)], f_send)

    @pl.when(is_owner)
    def _():
        drain(msgb.at[pl.ds(0, (WIDTH - 1) * 16)], b_send)
        drain(hbuf.at[pl.ds(0, (WIDTH - 1) * 8)], h_send)
        drain(inb, b_recv)
        drain(inh, h_recv)

    @pl.when(jnp.logical_not(is_owner))
    def _():
        drain(msgb, b_send)
        drain(hbuf, h_send)


def channel_kernel(
    inb, inh, w1, w1t, w2, w2c, twr, twi, outb, outh, sbuf, dcat, ybuf, zcat, spec, qbuf, rcat, obuf
):
    seq = lax.axis_index("seq")
    ch = lax.axis_index("ch")

    def chunks(body):
        @pl.loop(0, 8)
        def _(step):
            body(pl.ds(pl.multiple_of(step * 32, 32), 32), step)

    def after(rows, base, step):
        return pl.ds(pl.multiple_of(base + step * 32, 32), 32)

    def put(ref, rows_list, columns_list, high, low):
        ref[rows_list[0], columns_list[0]] = high
        ref[rows_list[1], columns_list[1]] = low
        ref[rows_list[2], columns_list[2]] = high

    def forward(count, slot):
        width = 256 * count
        ybuf[:, pl.ds(0, width)] = jnp.dot(
            w1[...], dcat[:, pl.ds(0, width)], preferred_element_type=F32
        )
        for index in range(count):
            columns = pl.ds(index * 256, 256)

            def body(rows, step):
                re, im = ybuf[rows, columns], ybuf[after(rows, 256, step), columns]
                cr, ci = twr[rows, :], twi[rows, :]
                place = after(rows, index * 256, step)
                for base, value in ((0, re * cr - im * ci), (256, re * ci + im * cr)):
                    high, low = halves(value)
                    put(
                        zcat,
                        (place,) * 3,
                        tuple(pl.ds(base + 512 * k, 256) for k in range(3)),
                        high,
                        low,
                    )

            chunks(body)
        spec[pl.ds(slot * 256, width), :] = jnp.dot(
            zcat[pl.ds(0, width), :], w2[...], preferred_element_type=F32
        )

    def inverse(pairs):
        count = len(pairs)
        width = 256 * count
        for index, (left, right, conj) in enumerate(pairs):

            def body(rows, step):
                a, b = after(rows, left * 256, step), after(rows, right * 256, step)
                ar, ai = spec[a, pl.ds(0, 256)], spec[a, pl.ds(256, 256)]
                br, bi = spec[b, pl.ds(0, 256)], spec[b, pl.ds(256, 256)]
                if conj:
                    re, im = ar * br + ai * bi, ai * br - ar * bi
                else:
                    re, im = ar * br - ai * bi, ai * br + ar * bi
                place = after(rows, index * 256, step)
                for base, value in ((0, re), (256, im)):
                    high, low = halves(value)
                    put(
                        zcat,
                        (place,) * 3,
                        tuple(pl.ds(base + 512 * k, 256) for k in range(3)),
                        high,
                        low,
                    )

            chunks(body)
        qbuf[pl.ds(0, width), :] = jnp.dot(
            zcat[pl.ds(0, width), :], w2c[...], preferred_element_type=F32
        )
        for index in range(count):
            columns = pl.ds(index * 256, 256)

            def body(rows, step):
                place = after(rows, index * 256, step)
                re, im = qbuf[place, pl.ds(0, 256)], qbuf[place, pl.ds(256, 256)]
                cr, ci = twr[rows, :], twi[rows, :]
                for base, value in ((0, re * cr + im * ci), (256, im * cr - re * ci)):
                    high, low = halves(value)
                    put(
                        rcat,
                        tuple(after(rows, base + 512 * k, step) for k in range(3)),
                        (columns,) * 3,
                        high,
                        low,
                    )

            chunks(body)
        obuf[:, pl.ds(0, width)] = jnp.dot(
            w1t[...], rcat[:, pl.ds(0, width)], preferred_element_type=F32
        )

    def load(ref, stride, array, half):
        return jnp.concatenate(
            [
                ref[pl.ds(array * 4 + 2 * half + part, SEQ, stride=stride), :]
                for part in range(2)
            ],
            1,
        )

    def place(half, index, value):
        high, low = halves(value)
        put(
            dcat,
            tuple(pl.ds(256 * k + half * 128, 128) for k in range(3)),
            (pl.ds(index * 256, 256),) * 3,
            high,
            low,
        )

    def block(half, index):
        return obuf[pl.ds(half * 128, 128), pl.ds(index * 256, 256)]

    def store(ref, stride, array, half, value):
        for part in range(2):
            ref[pl.ds(array * 4 + 2 * half + part, SEQ, stride=stride), :] = value[
                :, part * 128 : (part + 1) * 128
            ]

    @pl.when(owner_of(lax.div(seq, 8), ch) == seq)
    def _():
        sbuf[...] = inb[...].astype(F32)
        for half in range(2):
            place(half, 0, load(sbuf, 16, 0, half))
            place(half, 1, load(inh, 8, 0, half))
            place(half, 2, load(sbuf, 16, 2, half) * load(sbuf, 16, 3, half))
            place(half, 3, load(inh, 8, 1, half))
        forward(4, 0)
        inverse(((0, 1, False), (2, 3, True)))
        for half in range(2):
            gate = load(sbuf, 16, 1, half)
            first_u, grad_z = block(half, 0), block(half, 1)
            place(half, 0, gate * first_u)
            place(half, 1, gate * grad_z)
            store(sbuf, 16, 1, half, first_u * grad_z)
        forward(2, 4)
        inverse(((5, 1, True), (4, 3, False), (5, 0, True), (2, 4, True)))
        for half in range(2):
            store(sbuf, 16, 0, half, block(half, 0))
            store(sbuf, 16, 2, half, load(sbuf, 16, 3, half) * block(half, 1))
            store(outh, 8, 0, half, block(half, 2))
            store(outh, 8, 1, half, block(half, 3))
        outb[...] = sbuf[...].astype(BF16)


def outbound_kernel(
    outb,
    outh,
    feat,
    readout,
    windows,
    gotb,
    hidden_out,
    readout_out,
    goth,
    part_f,
    got_f,
    part_w,
    got_w,
    sum_w,
    got_v,
    b_send,
    b_recv,
    h_send,
    h_recv,
    f_send,
    f_recv,
    w_send,
    w_recv,
    v_send,
    v_recv,
):
    seq = lax.axis_index("seq")
    ch = lax.axis_index("ch")
    channel = lax.div(seq, 8)
    low = lax.rem(seq, 8)
    is_owner = owner_of(channel, ch) == seq
    barrier = pltpu.get_barrier_semaphore()
    peers = CH - 1 + 15 + 7

    @pl.loop(0, WIDTH)
    def _(other):
        owner = owner_of(other, ch)

        @pl.when(owner != seq)
        def _():
            greet(barrier, owner, ch)

    for step in range(1, CH):
        greet(barrier, seq, lax.rem(ch + step, CH))

    @pl.loop(1, 16)
    def _(step):
        greet(barrier, lax.rem(channel + step, 16) * 8 + low, ch)

    @pl.loop(1, 8)
    def _(step):
        greet(barrier, channel * 8 + lax.rem(low + step, 8), ch)

    @pl.when(is_owner)
    def _():
        pl.semaphore_wait(barrier, SEQ - 1 + peers)

        @pl.loop(1, SEQ)
        def _(step):
            to = lax.rem(seq + step, SEQ)
            send(
                outh.at[tile_rows(to, 8)], goth.at[tile_rows(channel, 8)], h_send, h_recv, to, ch
            )

        @pl.loop(1, SEQ)
        def _(step):
            to = lax.rem(seq + step, SEQ)
            send(
                outb.at[tile_rows(to, 16)], gotb.at[tile_rows(channel, 16)], b_send, b_recv, to, ch
            )

        pltpu.make_async_copy(
            outh.at[tile_rows(seq, 8)], goth.at[tile_rows(channel, 8)], h_recv
        ).start()
        pltpu.make_async_copy(
            outb.at[tile_rows(seq, 16)], gotb.at[tile_rows(channel, 16)], b_recv
        ).start()

    @pl.when(jnp.logical_not(is_owner))
    def _():
        pl.semaphore_wait(barrier, peers)

    drain(goth, h_recv)
    rows = [
        jnp.concatenate(
            [goth[pl.ds(order * 4 + part, WIDTH, stride=8), :] for part in range(4)], 1
        )
        for order in range(2)
    ]
    dhw = jnp.concatenate(rows, 0) * windows[...] * (1.0 / math.sqrt(SEQ * LOCUS))
    full = feat[...].astype(F32)
    highest = lax.Precision.HIGHEST
    part_f[...] = lax.dot_general(
        readout[...], dhw, (((0,), (0,)), ((), ())), precision=highest, preferred_element_type=F32
    )
    for step in range(1, CH):
        to = lax.rem(ch + step, CH)
        send(
            part_f.at[tile_rows(to, WIDTH)], got_f.at[tile_rows(ch, WIDTH)], f_send, f_recv, seq, to
        )
    grads = lax.dot_general(
        dhw, full, (((1,), (1,)), ((), ())), precision=highest, preferred_element_type=F32
    )
    part_w[...] = jnp.concatenate([grads[:WIDTH], grads[WIDTH:]], 1)
    got_w[tile_rows(channel, 16), :] = part_w[...]
    got_f[tile_rows(ch, WIDTH), :] = part_f[tile_rows(ch, WIDTH), :]

    @pl.loop(1, 16)
    def _(step):
        to = lax.rem(channel + step, 16) * 8 + low
        send(part_w, got_w.at[tile_rows(channel, 16)], w_send, w_recv, to, ch)

    drain(got_w.at[pl.ds(0, 15 * 16)], w_recv)
    total = got_w[pl.ds(0, 16), :]
    for index in range(1, 16):
        total = total + got_w[pl.ds(16 * index, 16), :]
    sum_w[...] = total
    got_v[tile_rows(low, 16), :] = total

    @pl.loop(1, 8)
    def _(step):
        to = channel * 8 + lax.rem(low + step, 8)
        send(sum_w, got_v.at[tile_rows(low, 16)], v_send, v_recv, to, ch)

    drain(got_f.at[pl.ds(0, 3 * WIDTH)], f_recv)
    summed = got_f[pl.ds(0, WIDTH), :]
    for index in range(1, CH):
        summed = summed + got_f[pl.ds(WIDTH * index, WIDTH), :]
    hidden_out[...] = summed.astype(BF16)
    drain(got_v.at[pl.ds(0, 7 * 16)], v_recv)
    total = got_v[pl.ds(0, 16), :]
    for index in range(1, 8):
        total = total + got_v[pl.ds(16 * index, 16), :]
    readout_out[...] = total.astype(BF16)
    drain(gotb, b_recv)
    drain(got_f.at[pl.ds(0, 3 * WIDTH)], f_send)
    drain(got_w.at[pl.ds(0, 15 * 16)], w_send)
    drain(got_v.at[pl.ds(0, 7 * 16)], v_send)

    @pl.when(is_owner)
    def _():
        drain(outh.at[pl.ds(0, (SEQ - 1) * 8)], h_send)
        drain(outb.at[pl.ds(0, (SEQ - 1) * 16)], b_send)


def vmem(count):
    return [pl.BlockSpec(memory_space=pltpu.VMEM)] * count


def shape(dims, dtype):
    return jax.ShapeDtypeStruct(dims, dtype)


def params(collective):
    return pltpu.CompilerParams(
        collective_id=collective, has_side_effects=True, vmem_limit_bytes=48 * 2**20
    )


def channel_call(inb, inh):
    return pl.pallas_call(
        channel_kernel,
        out_shape=(shape((2048, 128), BF16), shape((1024, 128), F32)),
        in_specs=vmem(8),
        out_specs=tuple(vmem(2)),
        scratch_shapes=[
            pltpu.VMEM((2048, 128), F32),
            pltpu.VMEM((768, 1024), BF16),
            pltpu.VMEM((512, 1024), F32),
            pltpu.VMEM((1024, 1536), BF16),
            pltpu.VMEM((1536, 512), F32),
            pltpu.VMEM((1024, 512), F32),
            pltpu.VMEM((1536, 1024), BF16),
            pltpu.VMEM((256, 1024), F32),
        ],
        compiler_params=pltpu.CompilerParams(vmem_limit_bytes=48 * 2**20),
    )(inb, inh, *[jnp.asarray(table) for table in make_tables()])


def body(
    signal_branch,
    leading_multiplier,
    trailing_multiplier,
    loss_upstream_adjoint,
    kernel_net_hidden,
    kernel_readout_matrix,
    kernel_attenuation,
):
    dma = pltpu.SemaphoreType.DMA
    seq_index = lax.axis_index("seq")
    position = (seq_index * LOCUS + jnp.arange(LOCUS, dtype=jnp.int32)).astype(F32)
    window = jnp.exp(-kernel_attenuation[:, :, None] * position)
    scale = jnp.sqrt(
        jnp.expm1(-2.0 * kernel_attenuation) / jnp.expm1(-2.0 * kernel_attenuation * (SEQ * LOCUS))
    )
    windows = (window * scale[:, :, None]).reshape(2 * WIDTH, LOCUS)
    readout = kernel_readout_matrix.reshape(2 * WIDTH, CH * WIDTH)
    msgb = jnp.stack(
        [signal_branch, leading_multiplier, trailing_multiplier, loss_upstream_adjoint], 1
    ).reshape(WIDTH * 16, 128)
    inb, inh, feat = pl.pallas_call(
        inbound_kernel,
        out_shape=(shape((2048, 128), BF16), shape((1024, 128), F32), shape((64, LOCUS), BF16)),
        in_specs=vmem(4),
        out_specs=tuple(vmem(3)),
        scratch_shapes=[pltpu.VMEM((WIDTH * 8, 128), F32)] + [dma] * 6,
        compiler_params=params(1),
    )(msgb, kernel_net_hidden, readout, windows)
    outb, outh = channel_call(inb, inh)
    gotb, hidden_grad, readout_grad = pl.pallas_call(
        outbound_kernel,
        out_shape=(
            shape((WIDTH * 16, 128), BF16),
            shape((WIDTH, LOCUS), BF16),
            shape((WIDTH, 128), BF16),
        ),
        in_specs=vmem(5),
        out_specs=tuple(vmem(3)),
        scratch_shapes=[
            pltpu.VMEM((WIDTH * 8, 128), F32),
            pltpu.VMEM((64, LOCUS), F32),
            pltpu.VMEM((64, LOCUS), F32),
            pltpu.VMEM((16, 128), F32),
            pltpu.VMEM((256, 128), F32),
            pltpu.VMEM((16, 128), F32),
            pltpu.VMEM((128, 128), F32),
        ]
        + [dma] * 10,
        compiler_params=params(2),
    )(outb, outh, feat, readout, windows)
    pieces = gotb.reshape(WIDTH, 4, LOCUS)
    return (
        pieces[:, 0],
        pieces[:, 1],
        pieces[:, 2],
        readout_grad.reshape(WIDTH, 2, 64).transpose(1, 0, 2),
        hidden_grad,
    )


def solution(mesh):
    in_specs = (
        P("ch", "seq"),
        P("ch", "seq"),
        P("ch", "seq"),
        P("ch", "seq"),
        P("ch", "seq"),
        P(None, "ch", None),
        P(None, "ch"),
    )
    out_specs = (
        P("ch", "seq"),
        P("ch", "seq"),
        P("ch", "seq"),
        P(None, "ch", None),
        P("ch", "seq"),
    )
    return jax.shard_map(body, mesh=mesh, in_specs=in_specs, out_specs=out_specs, check_vma=False)
```

```python
import math

import jax
import jax.numpy as jnp
import ml_dtypes
import numpy as np
from jax import lax
from jax.experimental import pallas as pl
from jax.experimental.pallas import tpu as pltpu
from jax.sharding import PartitionSpec as P

F32 = jnp.float32
BF16 = jnp.bfloat16
SEQ = 128
CH = 4
WIDTH = 16
LOCUS = 512
MESH = pl.DeviceIdType.MESH


def owner_of(channel, group):
    high = lax.rem(lax.div(channel, 4) + lax.rem(channel, 4) + group, 4)
    return channel * 8 + 2 * high


def halves(value):
    high = value.astype(BF16)
    return high, (value - high.astype(F32)).astype(BF16)


def np_halves(value):
    value = value.astype(np.float32)
    high = value.astype(ml_dtypes.bfloat16)
    return high, (value - high.astype(np.float32)).astype(ml_dtypes.bfloat16)


def make_tables():
    length = SEQ * LOCUS
    points = 2 * length
    order = np.concatenate([2 * np.arange(128), 2 * np.arange(128) + 1])
    coarse = np.arange(256) + 0.5
    angle = 2.0 * np.pi * coarse[:, None] * order[None, :] / 512.0
    first = np.concatenate([np.cos(angle), -np.sin(angle)], 0)
    first_hi, first_lo = np_halves(first)
    w1 = np.concatenate([first_hi, first_hi, first_lo], 1)
    last_hi, last_lo = np_halves(first.T / length)
    w1t = np.concatenate([last_hi, last_hi, last_lo], 1)
    fine = np.arange(256)
    angle = 2.0 * np.pi * (fine[:, None] * fine[None, :] % 256) / 256.0
    cos, sin = np.cos(angle), np.sin(angle)
    mid_hi, mid_lo = np_halves(np.block([[cos, -sin], [sin, cos]]))
    w2 = np.concatenate([mid_hi, mid_hi, mid_lo], 0)
    back_hi, back_lo = np_halves(np.block([[cos, sin], [-sin, cos]]))
    w2c = np.concatenate([back_hi, back_hi, back_lo], 0)
    angle = 2.0 * np.pi * coarse[:, None] * fine[None, :] / points
    return w1, w1t, w2, w2c, np.cos(angle).astype(np.float32), -np.sin(angle).astype(np.float32)


def tile_rows(index, count):
    return pl.ds(pl.multiple_of(index * count, count), count)


def send(src, dst, send_sem, recv_sem, seq, ch):
    pltpu.make_async_remote_copy(
        src_ref=src,
        dst_ref=dst,
        send_sem=send_sem,
        recv_sem=recv_sem,
        device_id=(seq, ch),
        device_id_type=MESH,
    ).start()


def drain(ref, sem):
    pltpu.make_async_copy(ref, ref, sem).wait()


def greet(barrier, seq, ch):
    pl.semaphore_signal(barrier, inc=1, device_id=(seq, ch), device_id_type=MESH)


def fused_kernel(
    branch,
    gate_a,
    gate_b,
    upstream,
    hidden,
    readout,
    windows,
    w1_hbm,
    w1t_hbm,
    w2_hbm,
    w2c_hbm,
    twr_hbm,
    twi_hbm,
    branch_out,
    gate_a_out,
    gate_b_out,
    readout_out,
    hidden_out,
    w1,
    w1t,
    w2,
    w2c,
    twr,
    twi,
    feat,
    stage,
    msg,
    inb,
    sbuf,
    gate,
    cross,
    dcat,
    ybuf,
    zcat,
    spec,
    qbuf,
    rcat,
    obuf,
    outb,
    got,
    part_f,
    got_f,
    part_w,
    got_w,
    sum_w,
    got_v,
    t_sem,
    f_send,
    f_recv,
    b_send,
    b_recv,
    g_send,
    g_recv,
    c_send,
    c_recv,
    s_send,
    s_recv,
    o_send,
    o_recv,
    p_send,
    p_recv,
    w_send,
    w_recv,
    v_send,
    v_recv,
):
    seq = lax.axis_index("seq")
    ch = lax.axis_index("ch")
    channel = lax.div(seq, 8)
    low = lax.rem(seq, 8)
    role = lax.rem(seq, 2)
    is_owner = owner_of(channel, ch) == seq - role
    partner = seq + 1 - 2 * role
    barrier = pltpu.get_barrier_semaphore()
    peers = CH - 1 + 15 + 7

    @pl.loop(0, WIDTH)
    def _(other):
        for core in range(2):
            owner = owner_of(other, ch) + core

            @pl.when(owner != seq)
            def _():
                greet(barrier, owner, ch)

    for step in range(1, CH):
        greet(barrier, seq, lax.rem(ch + step, CH))

    @pl.loop(1, 16)
    def _(step):
        greet(barrier, lax.rem(channel + step, 16) * 8 + low, ch)

    @pl.loop(1, 8)
    def _(step):
        greet(barrier, channel * 8 + lax.rem(low + step, 8), ch)

    tables = [
        (w1_hbm, w1),
        (w1t_hbm, w1t),
        (w2_hbm, w2),
        (w2c_hbm, w2c),
        (twr_hbm, twr),
        (twi_hbm, twi),
    ]

    @pl.when(is_owner)
    def _():
        @pl.loop(1, SEQ)
        def _(step):
            greet(barrier, lax.rem(seq + step, SEQ), ch)

        for index, (source, target) in enumerate(tables):
            pltpu.make_async_copy(source, target, t_sem.at[index]).start()

    def stage_rows(row, value):
        for part in range(4):
            stage[pl.ds(row + part, WIDTH, stride=16), :] = value[:, part * 128 : (part + 1) * 128]

    stage_rows(0, branch[...].astype(F32))
    stage_rows(4, gate_a[...].astype(F32))
    stage_rows(256, gate_b[...].astype(F32))
    stage_rows(260, upstream[...].astype(F32))

    @pl.when(is_owner)
    def _():
        pl.semaphore_wait(barrier, SEQ - 1 + 2 * WIDTH - 1 + peers)

    @pl.when(jnp.logical_not(is_owner))
    def _():
        pl.semaphore_wait(barrier, 2 * WIDTH + peers)

    mine = tile_rows(ch, WIDTH)
    for step in range(1, CH):
        send(hidden, feat.at[mine], f_send, f_recv, seq, lax.rem(ch + step, CH))
    feat[mine, :] = hidden[...]
    drain(feat.at[pl.ds(0, 3 * WIDTH)], f_recv)
    weight = readout[...]
    high, rest = halves(weight)
    middle, last = halves(weight - high.astype(F32))
    triple = jnp.dot(
        jnp.concatenate([high, middle, last], 0), feat[...], preferred_element_type=F32
    )
    filt = (triple[:32] + triple[32:64] + triple[64:]) * windows[...]
    for order in range(2):
        value = filt[order * WIDTH : (order + 1) * WIDTH]
        first = value.astype(BF16).astype(F32)
        stage_rows(order * 256 + 8, first)
        stage_rows(order * 256 + 12, value - first)
    msg[...] = stage[...].astype(BF16)
    slot = tile_rows(seq, 16)

    @pl.loop(0, WIDTH)
    def _(step):
        to = lax.rem(channel + step, WIDTH)
        for core in range(2):
            owner = owner_of(to, ch) + core
            piece = msg.at[tile_rows(core * WIDTH + to, 16)]

            @pl.when(owner != seq)
            def _():
                send(piece, inb.at[slot], b_send, b_recv, owner, ch)

            @pl.when(owner == seq)
            def _():
                pltpu.make_async_copy(piece, inb.at[slot], b_recv).start()

    def chunks(body):
        @pl.loop(0, 8)
        def _(step):
            body(pl.ds(pl.multiple_of(step * 32, 32), 32), step)

    def after(base, step):
        return pl.ds(pl.multiple_of(base + step * 32, 32), 32)

    def put_rows(place, base, value):
        high, low = halves(value)
        zcat[place, pl.ds(base, 256)] = high
        zcat[place, pl.ds(base + 512, 256)] = low
        zcat[place, pl.ds(base + 1024, 256)] = high

    def forward(count, slot):
        width = 256 * count
        ybuf[:, pl.ds(0, width)] = jnp.dot(
            w1[...], dcat[:, pl.ds(0, width)], preferred_element_type=F32
        )
        for index in range(count):
            columns = pl.ds(index * 256, 256)

            def body(rows, step):
                re, im = ybuf[rows, columns], ybuf[after(256, step), columns]
                cr, ci = twr[rows, :], twi[rows, :]
                place = after(index * 256, step)
                put_rows(place, 0, re * cr - im * ci)
                put_rows(place, 256, re * ci + im * cr)

            chunks(body)
        spec[pl.ds(slot * 256, width), :] = jnp.dot(
            zcat[pl.ds(0, width), :], w2[...], preferred_element_type=F32
        )

    def inverse(pairs):
        count = len(pairs)
        width = 256 * count
        for index, (left, right, sign, flip) in enumerate(pairs):

            def body(rows, step):
                a, b = after(left * 256, step), after(right * 256, step)
                ar, ai = spec[a, pl.ds(0, 256)], spec[a, pl.ds(256, 256)]
                br, bi = spec[b, pl.ds(0, 256)], spec[b, pl.ds(256, 256)] * sign
                place = after(index * 256, step)
                put_rows(place, 0, ar * br - ai * bi)
                put_rows(place, 256, (ar * bi + ai * br) * flip)

            chunks(body)
        qbuf[pl.ds(0, width), :] = jnp.dot(
            zcat[pl.ds(0, width), :], w2c[...], preferred_element_type=F32
        )
        for index in range(count):
            columns = pl.ds(index * 256, 256)

            def body(rows, step):
                place = after(index * 256, step)
                re, im = qbuf[place, pl.ds(0, 256)], qbuf[place, pl.ds(256, 256)]
                cr, ci = twr[rows, :], twi[rows, :]
                for base, value in ((0, re * cr + im * ci), (256, im * cr - re * ci)):
                    high, low = halves(value)
                    rcat[after(base, step), columns] = high
                    rcat[after(base + 512, step), columns] = low
                    rcat[after(base + 1024, step), columns] = high

            chunks(body)
        obuf[:, pl.ds(0, width)] = jnp.dot(
            w1t[...], rcat[:, pl.ds(0, width)], preferred_element_type=F32
        )

    def load(array, half):
        return jnp.concatenate(
            [sbuf[pl.ds(array * 4 + 2 * half + part, SEQ, stride=16), :] for part in range(2)], 1
        )

    def store(array, half, value):
        for part in range(2):
            sbuf[pl.ds(array * 4 + 2 * half + part, SEQ, stride=16), :] = value[
                :, part * 128 : (part + 1) * 128
            ]

    def place(half, index, high, low):
        columns = pl.ds(index * 256, 256)
        dcat[pl.ds(half * 128, 128), columns] = high
        dcat[pl.ds(256 + half * 128, 128), columns] = low
        dcat[pl.ds(512 + half * 128, 128), columns] = high

    def block(half, index):
        return obuf[pl.ds(half * 128, 128), pl.ds(index * 256, 256)]

    def swap(source, target, send_sem, recv_sem):
        return pltpu.make_async_remote_copy(
            src_ref=source,
            dst_ref=target,
            send_sem=send_sem,
            recv_sem=recv_sem,
            device_id=(partner, ch),
            device_id_type=MESH,
        )

    @pl.when(is_owner)
    def _():
        for index, (source, target) in enumerate(tables):
            pltpu.make_async_copy(source, target, t_sem.at[index]).wait()
        drain(inb, b_recv)
        first_core = role == 0
        sign = jnp.where(first_core, 1.0, -1.0).astype(F32)
        sbuf[...] = inb[...].astype(F32)
        for half in range(2):
            second = load(1, half)
            rows = pl.ds(half * 128, 128)
            place(half, 0, *halves(load(0, half) * jnp.where(first_core, 1.0, second)))
            place(half, 1, load(2, half).astype(BF16), load(3, half).astype(BF16))

            @pl.when(first_core)
            def _():
                gate[rows, :] = second

        @pl.when(first_core)
        def _():
            swap(gate, gate, g_send, g_recv).start()

        forward(2, 0)
        inverse(((0, 1, sign, 1.0),))

        @pl.when(first_core)
        def _():
            drain(gate, g_send)

        @pl.when(jnp.logical_not(first_core))
        def _():
            drain(gate, g_recv)

        for half in range(2):
            rows = pl.ds(half * 128, 128)
            value = block(half, 0)
            place(half, 0, *halves(gate[rows, :] * value))

            @pl.when(first_core)
            def _():
                store(3, half, value)

            @pl.when(jnp.logical_not(first_core))
            def _():
                cross[rows, :] = value

        @pl.when(jnp.logical_not(first_core))
        def _():
            swap(cross, cross, c_send, c_recv).start()

        forward(1, 2)
        mine = pl.ds(512, 256)
        theirs = pl.ds(768, 256)
        copy = swap(spec.at[mine], spec.at[theirs], s_send, s_recv)
        copy.start()
        copy.wait()
        inverse(((3, 1, -sign, 1.0), (3, 0, -1.0, sign)))

        @pl.when(first_core)
        def _():
            drain(cross, c_recv)
            for half in range(2):
                store(0, half, block(half, 0))
                store(1, half, load(3, half) * cross[pl.ds(half * 128, 128), :])

        @pl.when(jnp.logical_not(first_core))
        def _():
            drain(cross, c_send)
            for half in range(2):
                store(0, half, block(half, 0) * load(1, half))

        for half in range(2):
            value = block(half, 1)
            first = value.astype(BF16).astype(F32)
            store(2, half, first)
            store(3, half, value - first)
        outb[...] = sbuf[...].astype(BF16)
        home = tile_rows(role * WIDTH + channel, 16)

        @pl.loop(1, SEQ)
        def _(step):
            to = lax.rem(seq + step, SEQ)
            send(outb.at[tile_rows(to, 16)], got.at[home], o_send, o_recv, to, ch)

        pltpu.make_async_copy(outb.at[slot], got.at[home], o_recv).start()

    drain(got, o_recv)
    stage[...] = got[...].astype(F32)

    def taken(row):
        return jnp.concatenate(
            [stage[pl.ds(row + part, WIDTH, stride=16), :] for part in range(4)], 1
        )

    grads = jnp.concatenate([taken(8) + taken(12), taken(264) + taken(268)], 0)
    dhw = grads * windows[...] * (1.0 / math.sqrt(SEQ * LOCUS))
    dhi, dlo = halves(dhw)
    whi, wlo = high, middle
    part_f[...] = lax.dot_general(
        jnp.concatenate([whi, whi, wlo], 0),
        jnp.concatenate([dhi, dlo, dhi], 0),
        (((0,), (0,)), ((), ())),
        preferred_element_type=F32,
    )
    double = lax.dot_general(
        jnp.concatenate([dhi, dlo], 0),
        feat[...],
        (((1,), (1,)), ((), ())),
        preferred_element_type=F32,
    )
    total = double[:32] + double[32:]
    part_w[...] = jnp.concatenate([total[:WIDTH], total[WIDTH:]], 1)

    @pl.loop(1, 16)
    def _(step):
        to = lax.rem(channel + step, 16) * 8 + low
        send(part_w, got_w.at[tile_rows(channel, 16)], w_send, w_recv, to, ch)

    for step in range(1, CH):
        to = lax.rem(ch + step, CH)
        send(part_f.at[tile_rows(to, WIDTH)], got_f.at[mine], p_send, p_recv, seq, to)
    got_w[tile_rows(channel, 16), :] = part_w[...]
    got_f[mine, :] = part_f[mine, :]
    branch_out[...] = taken(0).astype(BF16)
    gate_a_out[...] = taken(4).astype(BF16)
    gate_b_out[...] = taken(256).astype(BF16)
    drain(got_w.at[pl.ds(0, 15 * 16)], w_recv)
    total = got_w[pl.ds(0, 16), :]
    for index in range(1, 16):
        total = total + got_w[pl.ds(16 * index, 16), :]
    sum_w[...] = total

    @pl.loop(1, 8)
    def _(step):
        to = channel * 8 + lax.rem(low + step, 8)
        send(sum_w, got_v.at[tile_rows(low, 16)], v_send, v_recv, to, ch)

    got_v[tile_rows(low, 16), :] = total
    drain(got_f.at[pl.ds(0, 3 * WIDTH)], p_recv)
    summed = got_f[pl.ds(0, WIDTH), :]
    for index in range(1, CH):
        summed = summed + got_f[pl.ds(WIDTH * index, WIDTH), :]
    hidden_out[...] = summed.astype(BF16)
    drain(feat.at[pl.ds(0, 3 * WIDTH)], f_send)
    drain(got_f.at[pl.ds(0, 3 * WIDTH)], p_send)
    drain(got_w.at[pl.ds(0, 15 * 16)], w_send)

    @pl.when(is_owner)
    def _():
        drain(msg.at[pl.ds(0, (2 * WIDTH - 1) * 16)], b_send)
        drain(outb.at[pl.ds(0, (SEQ - 1) * 16)], o_send)

    @pl.when(jnp.logical_not(is_owner))
    def _():
        drain(msg, b_send)

    drain(got_v.at[pl.ds(0, 7 * 16)], v_recv)
    total = got_v[pl.ds(0, 16), :]
    for index in range(1, 8):
        total = total + got_v[pl.ds(16 * index, 16), :]
    readout_out[...] = total.astype(BF16)
    drain(got_v.at[pl.ds(0, 7 * 16)], v_send)


def vmem(count):
    return [pl.BlockSpec(memory_space=pltpu.VMEM)] * count


def shape(dims, dtype):
    return jax.ShapeDtypeStruct(dims, dtype)


def body(
    signal_branch,
    leading_multiplier,
    trailing_multiplier,
    loss_upstream_adjoint,
    kernel_net_hidden,
    kernel_readout_matrix,
    kernel_attenuation,
):
    dma = pltpu.SemaphoreType.DMA
    seq_index = lax.axis_index("seq")
    position = (seq_index * LOCUS + jnp.arange(LOCUS, dtype=jnp.int32)).astype(F32)
    window = jnp.exp(-kernel_attenuation[:, :, None] * position)
    scale = jnp.sqrt(
        jnp.expm1(-2.0 * kernel_attenuation) / jnp.expm1(-2.0 * kernel_attenuation * (SEQ * LOCUS))
    )
    windows = (window * scale[:, :, None]).reshape(2 * WIDTH, LOCUS)
    readout = kernel_readout_matrix.reshape(2 * WIDTH, CH * WIDTH)
    tables = [jnp.asarray(table) for table in make_tables()]
    rows = shape((WIDTH, LOCUS), BF16)
    dv, da, db, readout_grad, hidden_grad = pl.pallas_call(
        fused_kernel,
        out_shape=(rows, rows, rows, shape((WIDTH, 128), BF16), rows),
        in_specs=vmem(7) + [pl.BlockSpec(memory_space=pl.ANY)] * 6,
        out_specs=tuple(vmem(5)),
        scratch_shapes=[pltpu.VMEM(table.shape, table.dtype) for table in tables]
        + [
            pltpu.VMEM((64, LOCUS), BF16),
            pltpu.VMEM((512, 128), F32),
            pltpu.VMEM((512, 128), BF16),
            pltpu.VMEM((2048, 128), BF16),
            pltpu.VMEM((2048, 128), F32),
            pltpu.VMEM((256, 256), F32),
            pltpu.VMEM((256, 256), F32),
            pltpu.VMEM((768, 512), BF16),
            pltpu.VMEM((512, 512), F32),
            pltpu.VMEM((512, 1536), BF16),
            pltpu.VMEM((1024, 512), F32),
            pltpu.VMEM((512, 512), F32),
            pltpu.VMEM((1536, 512), BF16),
            pltpu.VMEM((256, 512), F32),
            pltpu.VMEM((2048, 128), BF16),
            pltpu.VMEM((512, 128), BF16),
            pltpu.VMEM((64, LOCUS), F32),
            pltpu.VMEM((64, LOCUS), F32),
            pltpu.VMEM((16, 128), F32),
            pltpu.VMEM((256, 128), F32),
            pltpu.VMEM((16, 128), F32),
            pltpu.VMEM((128, 128), F32),
            pltpu.SemaphoreType.DMA((6,)),
        ]
        + [dma] * 18,
        compiler_params=pltpu.CompilerParams(
            collective_id=1, has_side_effects=True, vmem_limit_bytes=48 * 2**20
        ),
    )(
        signal_branch,
        leading_multiplier,
        trailing_multiplier,
        loss_upstream_adjoint,
        kernel_net_hidden,
        readout,
        windows,
        *tables,
    )
    return (dv, da, db, readout_grad.reshape(WIDTH, 2, 64).transpose(1, 0, 2), hidden_grad)


def solution(mesh):
    in_specs = (
        P("ch", "seq"),
        P("ch", "seq"),
        P("ch", "seq"),
        P("ch", "seq"),
        P("ch", "seq"),
        P(None, "ch", None),
        P(None, "ch"),
    )
    out_specs = (
        P("ch", "seq"),
        P("ch", "seq"),
        P("ch", "seq"),
        P(None, "ch", None),
        P("ch", "seq"),
    )
    return jax.shard_map(body, mesh=mesh, in_specs=in_specs, out_specs=out_specs, check_vma=False)
```

```python
import math

import jax
import jax.numpy as jnp
import ml_dtypes
import numpy as np
from jax import lax
from jax.experimental import pallas as pl
from jax.experimental.pallas import tpu as pltpu
from jax.sharding import PartitionSpec as P

F32 = jnp.float32
BF16 = jnp.bfloat16
SEQ = 128
CH = 4
WIDTH = 16
LOCUS = 512
VMEM_BYTES = 60 * 2**20
MESH = pl.DeviceIdType.MESH


def owner_of(channel, group):
    high = lax.rem(lax.div(channel, 4) + lax.rem(channel, 4) + 3 * group, 4)
    return channel * 8 + 2 * high


def less_one(value):
    near = jnp.ones_like(value)
    for term in range(11, 1, -1):
        near = 1.0 + near * value * (1.0 / term)
    return jnp.where(jnp.abs(value) < 0.5, near * value, jnp.exp(value) - 1.0)


def halves(value):
    high = value.astype(BF16)
    return high, (value - high.astype(F32)).astype(BF16)


def np_halves(value):
    value = value.astype(np.float32)
    high = value.astype(ml_dtypes.bfloat16)
    return high, (value - high.astype(np.float32)).astype(ml_dtypes.bfloat16)


def make_tables():
    length = SEQ * LOCUS
    points = 2 * length
    order = np.concatenate([2 * np.arange(128), 2 * np.arange(128) + 1])
    coarse = np.arange(256) + 0.5
    angle = 2.0 * np.pi * coarse[:, None] * order[None, :] / 512.0
    first = np.concatenate([np.cos(angle), -np.sin(angle)], 0)
    first_hi, first_lo = np_halves(first)
    w1 = np.concatenate([first_hi, first_hi, first_lo], 1)
    last_hi, last_lo = np_halves(first.T / length)
    w1t = np.concatenate([last_hi, last_hi, last_lo], 1)
    fine = np.arange(256)
    angle = 2.0 * np.pi * (fine[:, None] * fine[None, :] % 256) / 256.0
    cos, sin = np.cos(angle), np.sin(angle)
    mid_hi, mid_lo = np_halves(np.block([[cos, -sin], [sin, cos]]))
    w2 = np.concatenate([mid_hi, mid_hi, mid_lo], 0)
    back_hi, back_lo = np_halves(np.block([[cos, sin], [-sin, cos]]))
    w2c = np.concatenate([back_hi, back_hi, back_lo], 0)
    angle = 2.0 * np.pi * coarse[:, None] * fine[None, :] / points
    return w1, w1t, w2, w2c, np.cos(angle).astype(np.float32), -np.sin(angle).astype(np.float32)


def tile_rows(index, count):
    return pl.ds(pl.multiple_of(index * count, count), count)


def send(src, dst, send_sem, recv_sem, seq, ch):
    pltpu.make_async_remote_copy(
        src_ref=src,
        dst_ref=dst,
        send_sem=send_sem,
        recv_sem=recv_sem,
        device_id=(seq, ch),
        device_id_type=MESH,
    ).start()


def drain(ref, sem):
    pltpu.make_async_copy(ref, ref, sem).wait()


def greet(barrier, seq, ch):
    pl.semaphore_signal(barrier, inc=1, device_id=(seq, ch), device_id_type=MESH)


def fused_kernel(
    branch_hbm,
    gate_a_hbm,
    gate_b_hbm,
    upstream_hbm,
    hidden,
    readout_hbm,
    decay_hbm,
    w1_hbm,
    w1t_hbm,
    w2_hbm,
    w2c_hbm,
    twr_hbm,
    twi_hbm,
    packed,
    w1,
    w1t,
    w2,
    w2c,
    twr,
    twi,
    branch,
    gate_a,
    gate_b,
    upstream,
    readout,
    decay,
    windows,
    feat,
    stage,
    msg,
    inb,
    sbuf,
    gate,
    cross,
    dcat,
    ybuf,
    zcat,
    spec,
    qbuf,
    rcat,
    obuf,
    outb,
    got,
    part_f,
    got_f,
    part_w,
    got_w,
    sum_w,
    got_v,
    t_sem,
    a_sem,
    f_send,
    f_recv,
    b_send,
    b_recv,
    g_send,
    g_recv,
    c_send,
    c_recv,
    s_send,
    s_recv,
    o_send,
    o_recv,
    p_send,
    p_recv,
    w_send,
    w_recv,
    v_send,
    v_recv,
):
    seq = lax.axis_index("seq")
    ch = lax.axis_index("ch")
    channel = lax.div(seq, 8)
    low = lax.rem(seq, 8)
    role = lax.rem(seq, 2)
    is_owner = owner_of(channel, ch) == seq - role
    partner = seq + 1 - 2 * role
    barrier = pltpu.get_barrier_semaphore()
    mine = tile_rows(ch, WIDTH)

    for step in range(1, CH):
        greet(barrier, seq, lax.rem(ch + step, CH))

    arguments = [
        (hidden, feat.at[mine]),
        (branch_hbm, branch),
        (gate_a_hbm, gate_a),
        (gate_b_hbm, gate_b),
        (upstream_hbm, upstream),
        (readout_hbm, readout),
        (decay_hbm, decay),
    ]
    for index, (source, target) in enumerate(arguments):
        pltpu.make_async_copy(source, target, a_sem.at[index]).start()

    tables = [
        (w1_hbm, w1),
        (w1t_hbm, w1t),
        (w2_hbm, w2),
        (w2c_hbm, w2c),
        (twr_hbm, twr),
        (twi_hbm, twi),
    ]

    @pl.when(is_owner)
    def _():
        @pl.loop(1, SEQ)
        def _(step):
            greet(barrier, lax.rem(seq + step, SEQ), ch)

        for index, (source, target) in enumerate(tables):
            pltpu.make_async_copy(source, target, t_sem.at[index]).start()

    def stage_rows(row, value):
        for part in range(4):
            stage[pl.ds(row + part, WIDTH, stride=16), :] = value[:, part * 128 : (part + 1) * 128]

    for index, (source, target) in enumerate(arguments):
        pltpu.make_async_copy(source, target, a_sem.at[index]).wait()
    stage_rows(0, branch[...].astype(F32))
    stage_rows(4, gate_a[...].astype(F32))
    stage_rows(256, gate_b[...].astype(F32))
    stage_rows(260, upstream[...].astype(F32))
    rate = decay[...]
    scale = jnp.sqrt(less_one(-2.0 * rate) / less_one(-2.0 * rate * (SEQ * LOCUS)))
    diagonal = lax.broadcasted_iota(jnp.int32, (WIDTH, WIDTH), 0) == lax.broadcasted_iota(
        jnp.int32, (WIDTH, WIDTH), 1
    )
    position = (
        seq * LOCUS + lax.broadcasted_iota(jnp.int32, (WIDTH, LOCUS), 1)
    ).astype(F32)

    def column(values, order):
        return jnp.sum(jnp.where(diagonal, values[order : order + 1], 0.0), 1, keepdims=True)

    for order in range(2):
        windows[pl.ds(order * WIDTH, WIDTH), :] = jnp.exp(
            -column(rate, order) * position
        ) * column(scale, order)

    @pl.when(is_owner)
    def _():
        pl.semaphore_wait(barrier, 2 * WIDTH - 1 + CH - 1)

    @pl.when(jnp.logical_not(is_owner))
    def _():
        pl.semaphore_wait(barrier, 2 * WIDTH + CH - 1)

    for step in range(1, CH):
        send(hidden, feat.at[mine], f_send, f_recv, seq, lax.rem(ch + step, CH))
    drain(feat.at[pl.ds(0, 3 * WIDTH)], f_recv)
    weight = readout[...]
    high, rest = halves(weight)
    middle, last = halves(weight - high.astype(F32))
    triple = jnp.dot(
        jnp.concatenate([high, middle, last], 0), feat[...], preferred_element_type=F32
    )
    filt = (triple[:32] + triple[32:64] + triple[64:]) * windows[...]
    for order in range(2):
        value = filt[order * WIDTH : (order + 1) * WIDTH]
        first = value.astype(BF16).astype(F32)
        stage_rows(order * 256 + 8, first)
        stage_rows(order * 256 + 12, value - first)
    msg[...] = stage[...].astype(BF16)
    slot = tile_rows(seq, 16)

    @pl.loop(0, WIDTH)
    def _(step):
        to = lax.rem(channel + step, WIDTH)
        for core in range(2):
            owner = owner_of(to, ch) + core
            piece = msg.at[tile_rows(core * WIDTH + to, 16)]

            @pl.when(owner != seq)
            def _():
                send(piece, inb.at[slot], b_send, b_recv, owner, ch)

            @pl.when(owner == seq)
            def _():
                pltpu.make_async_copy(piece, inb.at[slot], b_recv).start()

    def chunks(body):
        @pl.loop(0, 8)
        def _(step):
            body(pl.ds(pl.multiple_of(step * 32, 32), 32), step)

    def after(base, step):
        return pl.ds(pl.multiple_of(base + step * 32, 32), 32)

    def put_rows(place, base, value):
        high, low = halves(value)
        zcat[place, pl.ds(base, 256)] = high
        zcat[place, pl.ds(base + 512, 256)] = low
        zcat[place, pl.ds(base + 1024, 256)] = high

    def forward(count, slot):
        width = 256 * count
        ybuf[:, pl.ds(0, width)] = jnp.dot(
            w1[...], dcat[:, pl.ds(0, width)], preferred_element_type=F32
        )
        for index in range(count):
            columns = pl.ds(index * 256, 256)

            def body(rows, step):
                re, im = ybuf[rows, columns], ybuf[after(256, step), columns]
                cr, ci = twr[rows, :], twi[rows, :]
                place = after(index * 256, step)
                put_rows(place, 0, re * cr - im * ci)
                put_rows(place, 256, re * ci + im * cr)

            chunks(body)
        spec[pl.ds(slot * 256, width), :] = jnp.dot(
            zcat[pl.ds(0, width), :], w2[...], preferred_element_type=F32
        )

    def inverse(pairs):
        count = len(pairs)
        width = 256 * count
        for index, (left, right, sign, flip) in enumerate(pairs):

            def body(rows, step):
                a, b = after(left * 256, step), after(right * 256, step)
                ar, ai = spec[a, pl.ds(0, 256)], spec[a, pl.ds(256, 256)]
                br, bi = spec[b, pl.ds(0, 256)], spec[b, pl.ds(256, 256)] * sign
                place = after(index * 256, step)
                put_rows(place, 0, ar * br - ai * bi)
                put_rows(place, 256, (ar * bi + ai * br) * flip)

            chunks(body)
        qbuf[pl.ds(0, width), :] = jnp.dot(
            zcat[pl.ds(0, width), :], w2c[...], preferred_element_type=F32
        )
        for index in range(count):
            columns = pl.ds(index * 256, 256)

            def body(rows, step):
                place = after(index * 256, step)
                re, im = qbuf[place, pl.ds(0, 256)], qbuf[place, pl.ds(256, 256)]
                cr, ci = twr[rows, :], twi[rows, :]
                for base, value in ((0, re * cr + im * ci), (256, im * cr - re * ci)):
                    high, low = halves(value)
                    rcat[after(base, step), columns] = high
                    rcat[after(base + 512, step), columns] = low
                    rcat[after(base + 1024, step), columns] = high

            chunks(body)
        obuf[:, pl.ds(0, width)] = jnp.dot(
            w1t[...], rcat[:, pl.ds(0, width)], preferred_element_type=F32
        )

    def load(array, half):
        return jnp.concatenate(
            [sbuf[pl.ds(array * 4 + 2 * half + part, SEQ, stride=16), :] for part in range(2)], 1
        )

    def store(array, half, value):
        for part in range(2):
            sbuf[pl.ds(array * 4 + 2 * half + part, SEQ, stride=16), :] = value[
                :, part * 128 : (part + 1) * 128
            ]

    def place(half, index, high, low):
        columns = pl.ds(index * 256, 256)
        dcat[pl.ds(half * 128, 128), columns] = high
        dcat[pl.ds(256 + half * 128, 128), columns] = low
        dcat[pl.ds(512 + half * 128, 128), columns] = high

    def block(half, index):
        return obuf[pl.ds(half * 128, 128), pl.ds(index * 256, 256)]

    def swap(source, target, send_sem, recv_sem):
        return pltpu.make_async_remote_copy(
            src_ref=source,
            dst_ref=target,
            send_sem=send_sem,
            recv_sem=recv_sem,
            device_id=(partner, ch),
            device_id_type=MESH,
        )

    @pl.when(is_owner)
    def _():
        for index, (source, target) in enumerate(tables):
            pltpu.make_async_copy(source, target, t_sem.at[index]).wait()
        drain(inb, b_recv)
        first_core = role == 0
        sign = jnp.where(first_core, 1.0, -1.0).astype(F32)
        sbuf[...] = inb[...].astype(F32)
        for half in range(2):
            second = load(1, half)
            rows = pl.ds(half * 128, 128)
            place(half, 0, *halves(load(0, half) * jnp.where(first_core, 1.0, second)))
            place(half, 1, load(2, half).astype(BF16), load(3, half).astype(BF16))

            @pl.when(first_core)
            def _():
                gate[rows, :] = second

        @pl.when(first_core)
        def _():
            swap(gate, gate, g_send, g_recv).start()

        forward(2, 0)
        inverse(((0, 1, sign, 1.0),))

        @pl.when(first_core)
        def _():
            drain(gate, g_send)

        @pl.when(jnp.logical_not(first_core))
        def _():
            drain(gate, g_recv)

        for half in range(2):
            rows = pl.ds(half * 128, 128)
            value = block(half, 0)
            place(half, 0, *halves(gate[rows, :] * value))

            @pl.when(first_core)
            def _():
                store(3, half, value)

            @pl.when(jnp.logical_not(first_core))
            def _():
                cross[rows, :] = value

        @pl.when(jnp.logical_not(first_core))
        def _():
            swap(cross, cross, c_send, c_recv).start()

        forward(1, 2)
        mine = pl.ds(512, 256)
        theirs = pl.ds(768, 256)
        copy = swap(spec.at[mine], spec.at[theirs], s_send, s_recv)
        copy.start()
        copy.wait()
        inverse(((3, 1, -sign, 1.0), (3, 0, -1.0, sign)))

        @pl.when(first_core)
        def _():
            drain(cross, c_recv)
            for half in range(2):
                store(0, half, block(half, 0))
                store(1, half, load(3, half) * cross[pl.ds(half * 128, 128), :])

        @pl.when(jnp.logical_not(first_core))
        def _():
            drain(cross, c_send)
            for half in range(2):
                store(0, half, block(half, 0) * load(1, half))

        for half in range(2):
            value = block(half, 1)
            first = value.astype(BF16).astype(F32)
            store(2, half, first)
            store(3, half, value - first)
        outb[...] = sbuf[...].astype(BF16)
        home = tile_rows(role * WIDTH + channel, 16)

        @pl.loop(1, SEQ)
        def _(step):
            to = lax.rem(seq + step, SEQ)
            send(outb.at[tile_rows(to, 16)], got.at[home], o_send, o_recv, to, ch)

        pltpu.make_async_copy(outb.at[slot], got.at[home], o_recv).start()

    drain(got, o_recv)
    stage[...] = got[...].astype(F32)

    def taken(row):
        return jnp.concatenate(
            [stage[pl.ds(row + part, WIDTH, stride=16), :] for part in range(4)], 1
        )

    grads = jnp.concatenate([taken(8) + taken(12), taken(264) + taken(268)], 0)
    dhw = grads * windows[...] * (1.0 / math.sqrt(SEQ * LOCUS))
    dhi, dlo = halves(dhw)
    whi, wlo = high, middle
    part_f[...] = lax.dot_general(
        jnp.concatenate([whi, whi, wlo], 0),
        jnp.concatenate([dhi, dlo, dhi], 0),
        (((0,), (0,)), ((), ())),
        preferred_element_type=F32,
    )
    double = lax.dot_general(
        jnp.concatenate([dhi, dlo], 0),
        feat[...],
        (((1,), (1,)), ((), ())),
        preferred_element_type=F32,
    )
    total = double[:32] + double[32:]
    part_w[...] = jnp.concatenate([total[:WIDTH], total[WIDTH:]], 1)

    @pl.loop(1, 16)
    def _(step):
        to = lax.rem(channel + step, 16) * 8 + low
        send(part_w, got_w.at[tile_rows(channel, 16)], w_send, w_recv, to, ch)

    for step in range(1, CH):
        to = lax.rem(ch + step, CH)
        send(part_f.at[tile_rows(to, WIDTH)], got_f.at[mine], p_send, p_recv, seq, to)
    got_w[tile_rows(channel, 16), :] = part_w[...]
    got_f[mine, :] = part_f[mine, :]
    packed[pl.ds(0, WIDTH), :] = taken(0).astype(BF16)
    packed[pl.ds(16, WIDTH), :] = taken(4).astype(BF16)
    packed[pl.ds(32, WIDTH), :] = taken(256).astype(BF16)
    drain(got_w.at[pl.ds(0, 15 * 16)], w_recv)
    total = got_w[pl.ds(0, 16), :]
    for index in range(1, 16):
        total = total + got_w[pl.ds(16 * index, 16), :]
    sum_w[...] = total

    @pl.loop(1, 8)
    def _(step):
        to = channel * 8 + lax.rem(low + step, 8)
        send(sum_w, got_v.at[tile_rows(low, 16)], v_send, v_recv, to, ch)

    got_v[tile_rows(low, 16), :] = total
    drain(got_f.at[pl.ds(0, 3 * WIDTH)], p_recv)
    summed = got_f[pl.ds(0, WIDTH), :]
    for index in range(1, CH):
        summed = summed + got_f[pl.ds(WIDTH * index, WIDTH), :]
    packed[pl.ds(48, WIDTH), :] = summed.astype(BF16)
    drain(feat.at[pl.ds(0, 3 * WIDTH)], f_send)
    drain(got_f.at[pl.ds(0, 3 * WIDTH)], p_send)
    drain(got_w.at[pl.ds(0, 15 * 16)], w_send)

    @pl.when(is_owner)
    def _():
        drain(msg.at[pl.ds(0, (2 * WIDTH - 1) * 16)], b_send)
        drain(outb.at[pl.ds(0, (SEQ - 1) * 16)], o_send)

    @pl.when(jnp.logical_not(is_owner))
    def _():
        drain(msg, b_send)

    drain(got_v.at[pl.ds(0, 7 * 16)], v_recv)
    total = got_v[pl.ds(0, 16), :]
    for index in range(1, 8):
        total = total + got_v[pl.ds(16 * index, 16), :]
    packed[pl.ds(64, 2 * WIDTH), pl.ds(0, 64)] = jnp.concatenate([total[:, :64], total[:, 64:]], 0).astype(BF16)
    drain(got_v.at[pl.ds(0, 7 * 16)], v_send)


def vmem(count):
    return [pl.BlockSpec(memory_space=pltpu.VMEM)] * count


def shape(dims, dtype):
    return jax.ShapeDtypeStruct(dims, dtype)


def body(
    signal_branch,
    leading_multiplier,
    trailing_multiplier,
    loss_upstream_adjoint,
    kernel_net_hidden,
    kernel_readout_matrix,
    kernel_attenuation,
):
    dma = pltpu.SemaphoreType.DMA
    readout = kernel_readout_matrix.reshape(2 * WIDTH, CH * WIDTH)
    tables = [jnp.asarray(table) for table in make_tables()]
    packed = pl.pallas_call(
        fused_kernel,
        out_shape=shape((96, LOCUS), BF16),
        in_specs=[pl.BlockSpec(memory_space=pltpu.HBM)] * 13,
        out_specs=vmem(1)[0],
        scratch_shapes=[pltpu.VMEM(table.shape, table.dtype) for table in tables]
        + [pltpu.VMEM((WIDTH, LOCUS), BF16)] * 4
        + [
            pltpu.VMEM((2 * WIDTH, 64), F32),
            pltpu.VMEM((2, WIDTH), F32),
            pltpu.VMEM((2 * WIDTH, LOCUS), F32),
            pltpu.VMEM((64, LOCUS), BF16),
            pltpu.VMEM((512, 128), F32),
            pltpu.VMEM((512, 128), BF16),
            pltpu.VMEM((2048, 128), BF16),
            pltpu.VMEM((2048, 128), F32),
            pltpu.VMEM((256, 256), F32),
            pltpu.VMEM((256, 256), F32),
            pltpu.VMEM((768, 512), BF16),
            pltpu.VMEM((512, 512), F32),
            pltpu.VMEM((512, 1536), BF16),
            pltpu.VMEM((1024, 512), F32),
            pltpu.VMEM((512, 512), F32),
            pltpu.VMEM((1536, 512), BF16),
            pltpu.VMEM((256, 512), F32),
            pltpu.VMEM((2048, 128), BF16),
            pltpu.VMEM((512, 128), BF16),
            pltpu.VMEM((64, LOCUS), F32),
            pltpu.VMEM((64, LOCUS), F32),
            pltpu.VMEM((16, 128), F32),
            pltpu.VMEM((256, 128), F32),
            pltpu.VMEM((16, 128), F32),
            pltpu.VMEM((128, 128), F32),
            pltpu.SemaphoreType.DMA((6,)),
            pltpu.SemaphoreType.DMA((7,)),
        ]
        + [dma] * 18,
        compiler_params=pltpu.CompilerParams(
            collective_id=1, has_side_effects=True, vmem_limit_bytes=VMEM_BYTES
        ),
    )(
        signal_branch,
        leading_multiplier,
        trailing_multiplier,
        loss_upstream_adjoint,
        kernel_net_hidden,
        readout,
        kernel_attenuation,
        *tables,
    )
    return (
        packed[:16],
        packed[16:32],
        packed[32:48],
        packed[64:, :64].reshape(2, WIDTH, 64),
        packed[48:64],
    )


def solution(mesh):
    in_specs = (
        P("ch", "seq"),
        P("ch", "seq"),
        P("ch", "seq"),
        P("ch", "seq"),
        P("ch", "seq"),
        P(None, "ch", None),
        P(None, "ch"),
    )
    out_specs = (
        P("ch", "seq"),
        P("ch", "seq"),
        P("ch", "seq"),
        P(None, "ch", None),
        P("ch", "seq"),
    )
    return jax.shard_map(body, mesh=mesh, in_specs=in_specs, out_specs=out_specs, check_vma=False)
```

```python
import math

import jax
import jax.numpy as jnp
import ml_dtypes
import numpy as np
from jax import lax
from jax.experimental import pallas as pl
from jax.experimental.pallas import tpu as pltpu
from jax.sharding import PartitionSpec as P

F32 = jnp.float32
BF16 = jnp.bfloat16
SEQ = 128
CH = 4
WIDTH = 16
LOCUS = 512
VMEM_BYTES = 60 * 2**20
MESH = pl.DeviceIdType.MESH


def owner_of(channel, group):
    high = lax.rem(lax.div(channel, 4) + lax.rem(channel, 4) + 3 * group, 4)
    return channel * 8 + 2 * high


def less_one(value):
    near = jnp.ones_like(value)
    for term in range(11, 1, -1):
        near = 1.0 + near * value * (1.0 / term)
    return jnp.where(jnp.abs(value) < 0.5, near * value, jnp.exp(value) - 1.0)


def halves(value):
    high = value.astype(BF16)
    return high, (value - high.astype(F32)).astype(BF16)


def np_halves(value):
    value = value.astype(np.float32)
    high = value.astype(ml_dtypes.bfloat16)
    return high, (value - high.astype(np.float32)).astype(ml_dtypes.bfloat16)


def make_tables():
    length = SEQ * LOCUS
    points = 2 * length
    order = np.concatenate([2 * np.arange(128), 2 * np.arange(128) + 1])
    coarse = np.arange(256) + 0.5
    angle = 2.0 * np.pi * coarse[:, None] * order[None, :] / 512.0
    first = np.concatenate([np.cos(angle), -np.sin(angle)], 0)
    first_hi, first_lo = np_halves(first)
    w1 = np.concatenate([first_hi, first_hi, first_lo], 1)
    last_hi, last_lo = np_halves(first.T / length)
    w1t = np.concatenate([last_hi, last_hi, last_lo], 1)
    fine = np.arange(256)
    angle = 2.0 * np.pi * (fine[:, None] * fine[None, :] % 256) / 256.0
    cos, sin = np.cos(angle), np.sin(angle)
    mid_hi, mid_lo = np_halves(np.block([[cos, -sin], [sin, cos]]))
    w2 = np.concatenate([mid_hi, mid_hi, mid_lo], 0)
    back_hi, back_lo = np_halves(np.block([[cos, sin], [-sin, cos]]))
    w2c = np.concatenate([back_hi, back_hi, back_lo], 0)
    angle = 2.0 * np.pi * coarse[:, None] * fine[None, :] / points
    return w1, w1t, w2, w2c, np.cos(angle).astype(np.float32), -np.sin(angle).astype(np.float32)


def tile_rows(index, count):
    return pl.ds(pl.multiple_of(index * count, count), count)


def send(src, dst, send_sem, recv_sem, seq, ch):
    pltpu.make_async_remote_copy(
        src_ref=src,
        dst_ref=dst,
        send_sem=send_sem,
        recv_sem=recv_sem,
        device_id=(seq, ch),
        device_id_type=MESH,
    ).start()


def drain(ref, sem):
    pltpu.make_async_copy(ref, ref, sem).wait()


def greet(barrier, seq, ch):
    pl.semaphore_signal(barrier, inc=1, device_id=(seq, ch), device_id_type=MESH)


def fused_kernel(
    branch_hbm,
    gate_a_hbm,
    gate_b_hbm,
    upstream_hbm,
    hidden,
    readout_hbm,
    decay_hbm,
    w1_hbm,
    w1t_hbm,
    w2_hbm,
    w2c_hbm,
    twr_hbm,
    twi_hbm,
    packed,
    w1,
    w1t,
    w2,
    w2c,
    twr,
    twi,
    branch,
    gate_a,
    gate_b,
    upstream,
    readout,
    decay,
    windows,
    feat,
    stage,
    msg,
    hmsg,
    inb,
    inh,
    sbuf,
    third,
    cross,
    dcat,
    ybuf,
    zcat,
    spec,
    qbuf,
    rcat,
    obuf,
    outb,
    outh,
    got,
    goth,
    part_f,
    got_f,
    part_w,
    got_w,
    sum_w,
    got_v,
    t_sem,
    a_sem,
    f_send,
    f_recv,
    b_send,
    b_recv,
    h_send,
    h_recv,
    g_send,
    g_recv,
    c_send,
    c_recv,
    s_send,
    s_recv,
    e_send,
    e_recv,
    o_send,
    o_recv,
    k_send,
    k_recv,
    p_send,
    p_recv,
    w_send,
    w_recv,
    v_send,
    v_recv,
):
    seq = lax.axis_index("seq")
    ch = lax.axis_index("ch")
    channel = lax.div(seq, 8)
    low = lax.rem(seq, 8)
    role = lax.rem(seq, 2)
    is_owner = owner_of(channel, ch) == seq - role
    partner = seq + 1 - 2 * role
    barrier = pltpu.get_barrier_semaphore()
    mine = tile_rows(ch, WIDTH)

    for step in range(1, CH):
        greet(barrier, seq, lax.rem(ch + step, CH))

    arguments = [
        (hidden, feat.at[mine]),
        (branch_hbm, branch),
        (gate_a_hbm, gate_a),
        (gate_b_hbm, gate_b),
        (upstream_hbm, upstream),
        (readout_hbm, readout),
        (decay_hbm, decay),
    ]
    for index, (source, target) in enumerate(arguments):
        pltpu.make_async_copy(source, target, a_sem.at[index]).start()

    tables = [
        (w1_hbm, w1),
        (w1t_hbm, w1t),
        (w2_hbm, w2),
        (w2c_hbm, w2c),
        (twr_hbm, twr),
        (twi_hbm, twi),
    ]

    @pl.when(is_owner)
    def _():
        @pl.loop(1, SEQ)
        def _(step):
            greet(barrier, lax.rem(seq + step, SEQ), ch)

        for index, (source, target) in enumerate(tables):
            pltpu.make_async_copy(source, target, t_sem.at[index]).start()

    def stage_rows(row, value):
        for part in range(4):
            stage[pl.ds(row + part, WIDTH, stride=16), :] = value[:, part * 128 : (part + 1) * 128]

    for index, (source, target) in enumerate(arguments):
        pltpu.make_async_copy(source, target, a_sem.at[index]).wait()
    stage_rows(0, branch[...].astype(F32))
    stage_rows(4, gate_a[...].astype(F32))
    stage_rows(8, gate_b[...].astype(F32))
    stage_rows(12, upstream[...].astype(F32))
    msg[...] = stage[...].astype(BF16)
    rate = decay[...]
    scale = jnp.sqrt(less_one(-2.0 * rate) / less_one(-2.0 * rate * (SEQ * LOCUS)))
    diagonal = lax.broadcasted_iota(jnp.int32, (WIDTH, WIDTH), 0) == lax.broadcasted_iota(
        jnp.int32, (WIDTH, WIDTH), 1
    )
    position = (
        seq * LOCUS + lax.broadcasted_iota(jnp.int32, (WIDTH, LOCUS), 1)
    ).astype(F32)

    def column(values, order):
        return jnp.sum(jnp.where(diagonal, values[order : order + 1], 0.0), 1, keepdims=True)

    for order in range(2):
        windows[pl.ds(order * WIDTH, WIDTH), :] = jnp.exp(
            -column(rate, order) * position
        ) * column(scale, order)

    @pl.when(is_owner)
    def _():
        pl.semaphore_wait(barrier, 2 * WIDTH - 1 + CH - 1)

    @pl.when(jnp.logical_not(is_owner))
    def _():
        pl.semaphore_wait(barrier, 2 * WIDTH + CH - 1)

    for step in range(1, CH):
        send(hidden, feat.at[mine], f_send, f_recv, seq, lax.rem(ch + step, CH))

    slot = tile_rows(seq, 16)

    @pl.loop(0, WIDTH)
    def _(step):
        to = lax.rem(channel + step, WIDTH)
        owner = owner_of(to, ch)
        piece = msg.at[tile_rows(to, 16)]

        @pl.when(owner != seq)
        def _():
            send(piece, inb.at[slot], b_send, b_recv, owner, ch)

        @pl.when(owner == seq)
        def _():
            pltpu.make_async_copy(piece, inb.at[slot], b_recv).start()

    drain(feat.at[pl.ds(0, 3 * WIDTH)], f_recv)
    weight = readout[...]
    high, rest = halves(weight)
    middle, last = halves(weight - high.astype(F32))
    triple = jnp.dot(
        jnp.concatenate([high, middle, last], 0), feat[...], preferred_element_type=F32
    )
    filt = (triple[:32] + triple[32:64] + triple[64:]) * windows[...]
    for order in range(2):
        for part in range(4):
            hmsg[pl.ds(order * 64 + part, WIDTH, stride=4), :] = filt[
                order * WIDTH : (order + 1) * WIDTH, part * 128 : (part + 1) * 128
            ]

    @pl.loop(0, WIDTH)
    def _(step):
        to = lax.rem(channel + step, WIDTH)
        for core in range(2):
            owner = owner_of(to, ch) + core
            piece = hmsg.at[tile_rows(core * WIDTH + to, 4)]

            @pl.when(owner != seq)
            def _():
                send(piece, inh.at[tile_rows(seq, 4)], h_send, h_recv, owner, ch)

            @pl.when(owner == seq)
            def _():
                pltpu.make_async_copy(piece, inh.at[tile_rows(seq, 4)], h_recv).start()

    def chunks(body):
        @pl.loop(0, 8)
        def _(step):
            body(pl.ds(pl.multiple_of(step * 32, 32), 32), step)

    def after(base, step):
        return pl.ds(pl.multiple_of(base + step * 32, 32), 32)

    def put_rows(place, base, value):
        high, low = halves(value)
        zcat[place, pl.ds(base, 256)] = high
        zcat[place, pl.ds(base + 512, 256)] = low
        zcat[place, pl.ds(base + 1024, 256)] = high

    def forward(count, slot):
        width = 256 * count
        ybuf[:, pl.ds(0, width)] = jnp.dot(
            w1[...], dcat[:, pl.ds(0, width)], preferred_element_type=F32
        )
        for index in range(count):
            columns = pl.ds(index * 256, 256)

            def body(rows, step):
                re, im = ybuf[rows, columns], ybuf[after(256, step), columns]
                cr, ci = twr[rows, :], twi[rows, :]
                place = after(index * 256, step)
                put_rows(place, 0, re * cr - im * ci)
                put_rows(place, 256, re * ci + im * cr)

            chunks(body)
        spec[pl.ds(slot * 256, width), :] = jnp.dot(
            zcat[pl.ds(0, width), :], w2[...], preferred_element_type=F32
        )

    def inverse(pairs):
        count = len(pairs)
        width = 256 * count
        for index, (left, right, sign, flip) in enumerate(pairs):

            def body(rows, step):
                a, b = after(left * 256, step), after(right * 256, step)
                ar, ai = spec[a, pl.ds(0, 256)], spec[a, pl.ds(256, 256)]
                br, bi = spec[b, pl.ds(0, 256)], spec[b, pl.ds(256, 256)] * sign
                place = after(index * 256, step)
                put_rows(place, 0, ar * br - ai * bi)
                put_rows(place, 256, (ar * bi + ai * br) * flip)

            chunks(body)
        qbuf[pl.ds(0, width), :] = jnp.dot(
            zcat[pl.ds(0, width), :], w2c[...], preferred_element_type=F32
        )
        for index in range(count):
            columns = pl.ds(index * 256, 256)

            def body(rows, step):
                place = after(index * 256, step)
                re, im = qbuf[place, pl.ds(0, 256)], qbuf[place, pl.ds(256, 256)]
                cr, ci = twr[rows, :], twi[rows, :]
                for base, value in ((0, re * cr + im * ci), (256, im * cr - re * ci)):
                    high, low = halves(value)
                    rcat[after(base, step), columns] = high
                    rcat[after(base + 512, step), columns] = low
                    rcat[after(base + 1024, step), columns] = high

            chunks(body)
        obuf[:, pl.ds(0, width)] = jnp.dot(
            w1t[...], rcat[:, pl.ds(0, width)], preferred_element_type=F32
        )

    def load(array, half):
        return jnp.concatenate(
            [sbuf[pl.ds(array * 4 + 2 * half + part, SEQ, stride=16), :] for part in range(2)], 1
        )

    def store(array, half, value):
        for part in range(2):
            sbuf[pl.ds(array * 4 + 2 * half + part, SEQ, stride=16), :] = value[
                :, part * 128 : (part + 1) * 128
            ]

    def place(half, index, high, low):
        columns = pl.ds(index * 256, 256)
        dcat[pl.ds(half * 128, 128), columns] = high
        dcat[pl.ds(256 + half * 128, 128), columns] = low
        dcat[pl.ds(512 + half * 128, 128), columns] = high

    def block(half, index):
        return obuf[pl.ds(half * 128, 128), pl.ds(index * 256, 256)]

    def swap(source, target, send_sem, recv_sem):
        return pltpu.make_async_remote_copy(
            src_ref=source,
            dst_ref=target,
            send_sem=send_sem,
            recv_sem=recv_sem,
            device_id=(partner, ch),
            device_id_type=MESH,
        )

    @pl.when(is_owner)
    def _():
        for index, (source, target) in enumerate(tables):
            pltpu.make_async_copy(source, target, t_sem.at[index]).wait()
        first_core = role == 0

        @pl.when(first_core)
        def _():
            drain(inb, b_recv)
            swap(inb, inb, g_send, g_recv).start()

        @pl.when(jnp.logical_not(first_core))
        def _():
            drain(inb, g_recv)

        sign = jnp.where(first_core, 1.0, -1.0).astype(F32)
        sbuf[...] = inb[...].astype(F32)
        for half in range(2):
            value = jnp.where(first_core, load(0, half), load(2, half) * load(3, half))
            place(half, 0, *halves(value))
        drain(inh, h_recv)
        for half in range(2):
            value = jnp.concatenate(
                [inh[pl.ds(2 * half + part, SEQ, stride=4), :] for part in range(2)], 1
            )
            place(half, 1, *halves(value))
        forward(2, 0)
        inverse(((0, 1, sign, 1.0),))

        for half in range(2):
            rows = pl.ds(half * 128, 128)
            value = block(half, 0)
            place(half, 0, *halves(load(1, half) * value))

            @pl.when(first_core)
            def _():
                store(3, half, value)

            @pl.when(jnp.logical_not(first_core))
            def _():
                cross[rows, :] = value

        @pl.when(jnp.logical_not(first_core))
        def _():
            swap(cross, cross, c_send, c_recv).start()

        forward(1, 2)
        mine = pl.ds(512, 256)
        theirs = pl.ds(768, 256)
        copy = swap(spec.at[mine], spec.at[theirs], s_send, s_recv)
        copy.start()
        copy.wait()
        inverse(((3, 1, -sign, 1.0), (3, 0, -1.0, sign)))

        for half in range(2):
            value = block(half, 1)
            for part in range(2):
                outh[pl.ds(2 * half + part, SEQ, stride=4), :] = value[
                    :, part * 128 : (part + 1) * 128
                ]
        home = role * WIDTH + channel

        @pl.loop(1, SEQ)
        def _(step):
            to = lax.rem(seq + step, SEQ)
            send(outh.at[tile_rows(to, 4)], goth.at[tile_rows(home, 4)], o_send, o_recv, to, ch)

        pltpu.make_async_copy(
            outh.at[tile_rows(seq, 4)], goth.at[tile_rows(home, 4)], o_recv
        ).start()

        @pl.when(jnp.logical_not(first_core))
        def _():
            for half in range(2):
                third[pl.ds(half * 128, 128), :] = block(half, 0) * load(3, half)
            swap(third, third, e_send, e_recv).start()

        @pl.when(first_core)
        def _():
            drain(cross, c_recv)
            for half in range(2):
                rows = pl.ds(half * 128, 128)
                store(0, half, block(half, 0))
                store(1, half, load(3, half) * cross[rows, :])
            drain(third, e_recv)
            for half in range(2):
                store(2, half, third[pl.ds(half * 128, 128), :])
            outb[...] = sbuf[...].astype(BF16)

            @pl.loop(1, SEQ)
            def _(step):
                to = lax.rem(seq + step, SEQ)
                send(
                    outb.at[tile_rows(to, 16)], got.at[tile_rows(channel, 16)], k_send, k_recv, to, ch
                )

            pltpu.make_async_copy(outb.at[slot], got.at[tile_rows(channel, 16)], k_recv).start()

    drain(goth, o_recv)
    grads = jnp.concatenate(
        [
            jnp.concatenate(
                [goth[pl.ds(order * 64 + part, WIDTH, stride=4), :] for part in range(4)], 1
            )
            for order in range(2)
        ],
        0,
    )
    dhw = grads * windows[...] * (1.0 / math.sqrt(SEQ * LOCUS))
    dhi, dlo = halves(dhw)
    whi, wlo = high, middle
    part_f[...] = lax.dot_general(
        jnp.concatenate([whi, whi, wlo], 0),
        jnp.concatenate([dhi, dlo, dhi], 0),
        (((0,), (0,)), ((), ())),
        preferred_element_type=F32,
    )
    double = lax.dot_general(
        jnp.concatenate([dhi, dlo], 0),
        feat[...],
        (((1,), (1,)), ((), ())),
        preferred_element_type=F32,
    )
    total = double[:32] + double[32:]
    part_w[...] = jnp.concatenate([total[:WIDTH], total[WIDTH:]], 1)

    @pl.loop(1, 16)
    def _(step):
        to = lax.rem(channel + step, 16) * 8 + low
        send(part_w, got_w.at[tile_rows(channel, 16)], w_send, w_recv, to, ch)

    for step in range(1, CH):
        to = lax.rem(ch + step, CH)
        send(part_f.at[tile_rows(to, WIDTH)], got_f.at[mine], p_send, p_recv, seq, to)
    got_w[tile_rows(channel, 16), :] = part_w[...]
    got_f[mine, :] = part_f[mine, :]
    drain(got_w.at[pl.ds(0, 15 * 16)], w_recv)
    total = got_w[pl.ds(0, 16), :]
    for index in range(1, 16):
        total = total + got_w[pl.ds(16 * index, 16), :]
    sum_w[...] = total

    @pl.loop(1, 8)
    def _(step):
        to = channel * 8 + lax.rem(low + step, 8)
        send(sum_w, got_v.at[tile_rows(low, 16)], v_send, v_recv, to, ch)

    got_v[tile_rows(low, 16), :] = total
    drain(got_f.at[pl.ds(0, 3 * WIDTH)], p_recv)
    summed = got_f[pl.ds(0, WIDTH), :]
    for index in range(1, CH):
        summed = summed + got_f[pl.ds(WIDTH * index, WIDTH), :]
    packed[pl.ds(48, WIDTH), :] = summed.astype(BF16)
    drain(got, k_recv)
    stage[...] = got[...].astype(F32)
    for index in range(3):
        packed[pl.ds(16 * index, WIDTH), :] = jnp.concatenate(
            [stage[pl.ds(4 * index + part, WIDTH, stride=16), :] for part in range(4)], 1
        ).astype(BF16)
    drain(feat.at[pl.ds(0, 3 * WIDTH)], f_send)
    drain(got_f.at[pl.ds(0, 3 * WIDTH)], p_send)
    drain(got_w.at[pl.ds(0, 15 * 16)], w_send)

    @pl.when(is_owner)
    def _():
        drain(hmsg.at[pl.ds(0, (2 * WIDTH - 1) * 4)], h_send)
        drain(outh.at[pl.ds(0, (SEQ - 1) * 4)], o_send)

        @pl.when(role == 0)
        def _():
            drain(msg.at[pl.ds(0, (WIDTH - 1) * 16)], b_send)
            drain(inb, g_send)
            drain(outb.at[pl.ds(0, (SEQ - 1) * 16)], k_send)

        @pl.when(role == 1)
        def _():
            drain(msg, b_send)
            drain(cross, c_send)
            drain(third, e_send)

    @pl.when(jnp.logical_not(is_owner))
    def _():
        drain(msg, b_send)
        drain(hmsg, h_send)

    drain(got_v.at[pl.ds(0, 7 * 16)], v_recv)
    total = got_v[pl.ds(0, 16), :]
    for index in range(1, 8):
        total = total + got_v[pl.ds(16 * index, 16), :]
    packed[pl.ds(64, 2 * WIDTH), pl.ds(0, 64)] = jnp.concatenate([total[:, :64], total[:, 64:]], 0).astype(BF16)
    drain(got_v.at[pl.ds(0, 7 * 16)], v_send)


def vmem(count):
    return [pl.BlockSpec(memory_space=pltpu.VMEM)] * count


def shape(dims, dtype):
    return jax.ShapeDtypeStruct(dims, dtype)


def body(
    signal_branch,
    leading_multiplier,
    trailing_multiplier,
    loss_upstream_adjoint,
    kernel_net_hidden,
    kernel_readout_matrix,
    kernel_attenuation,
):
    dma = pltpu.SemaphoreType.DMA
    readout = kernel_readout_matrix.reshape(2 * WIDTH, CH * WIDTH)
    tables = [jnp.asarray(table) for table in make_tables()]
    packed = pl.pallas_call(
        fused_kernel,
        out_shape=shape((96, LOCUS), BF16),
        in_specs=[pl.BlockSpec(memory_space=pltpu.HBM)] * 13,
        out_specs=vmem(1)[0],
        scratch_shapes=[pltpu.VMEM(table.shape, table.dtype) for table in tables]
        + [pltpu.VMEM((WIDTH, LOCUS), BF16)] * 4
        + [
            pltpu.VMEM((2 * WIDTH, 64), F32),
            pltpu.VMEM((2, WIDTH), F32),
            pltpu.VMEM((2 * WIDTH, LOCUS), F32),
            pltpu.VMEM((64, LOCUS), BF16),
            pltpu.VMEM((256, 128), F32),
            pltpu.VMEM((256, 128), BF16),
            pltpu.VMEM((128, 128), F32),
            pltpu.VMEM((2048, 128), BF16),
            pltpu.VMEM((512, 128), F32),
            pltpu.VMEM((2048, 128), F32),
            pltpu.VMEM((256, 256), F32),
            pltpu.VMEM((256, 256), F32),
            pltpu.VMEM((768, 512), BF16),
            pltpu.VMEM((512, 512), F32),
            pltpu.VMEM((512, 1536), BF16),
            pltpu.VMEM((1024, 512), F32),
            pltpu.VMEM((512, 512), F32),
            pltpu.VMEM((1536, 512), BF16),
            pltpu.VMEM((256, 512), F32),
            pltpu.VMEM((2048, 128), BF16),
            pltpu.VMEM((512, 128), F32),
            pltpu.VMEM((256, 128), BF16),
            pltpu.VMEM((128, 128), F32),
            pltpu.VMEM((64, LOCUS), F32),
            pltpu.VMEM((64, LOCUS), F32),
            pltpu.VMEM((16, 128), F32),
            pltpu.VMEM((256, 128), F32),
            pltpu.VMEM((16, 128), F32),
            pltpu.VMEM((128, 128), F32),
            pltpu.SemaphoreType.DMA((6,)),
            pltpu.SemaphoreType.DMA((7,)),
        ]
        + [dma] * 24,
        compiler_params=pltpu.CompilerParams(
            collective_id=1, has_side_effects=True, vmem_limit_bytes=VMEM_BYTES
        ),
    )(
        signal_branch,
        leading_multiplier,
        trailing_multiplier,
        loss_upstream_adjoint,
        kernel_net_hidden,
        readout,
        kernel_attenuation,
        *tables,
    )
    return (
        packed[:16],
        packed[16:32],
        packed[32:48],
        packed[64:, :64].reshape(2, WIDTH, 64),
        packed[48:64],
    )


def solution(mesh):
    in_specs = (
        P("ch", "seq"),
        P("ch", "seq"),
        P("ch", "seq"),
        P("ch", "seq"),
        P("ch", "seq"),
        P(None, "ch", None),
        P(None, "ch"),
    )
    out_specs = (
        P("ch", "seq"),
        P("ch", "seq"),
        P("ch", "seq"),
        P(None, "ch", None),
        P("ch", "seq"),
    )
    return jax.shard_map(body, mesh=mesh, in_specs=in_specs, out_specs=out_specs, check_vma=False)
```

```python
import math

import jax
import jax.numpy as jnp
import ml_dtypes
import numpy as np
from jax import lax
from jax.experimental import pallas as pl
from jax.experimental.pallas import tpu as pltpu
from jax.sharding import PartitionSpec as P

F32 = jnp.float32
BF16 = jnp.bfloat16
SEQ = 128
CH = 4
WIDTH = 16
LOCUS = 512
VMEM_BYTES = 60 * 2**20
MESH = pl.DeviceIdType.MESH


def owner_of(channel, group):
    high = lax.rem(lax.div(channel, 4) + lax.rem(channel, 4) + 3 * group, 4)
    return channel * 8 + 2 * high


def less_one(value):
    near = jnp.ones_like(value)
    for term in range(11, 1, -1):
        near = 1.0 + near * value * (1.0 / term)
    return jnp.where(jnp.abs(value) < 0.5, near * value, jnp.exp(value) - 1.0)


def halves(value):
    high = value.astype(BF16)
    return high, (value - high.astype(F32)).astype(BF16)


def np_halves(value):
    value = value.astype(np.float32)
    high = value.astype(ml_dtypes.bfloat16)
    return high, (value - high.astype(np.float32)).astype(ml_dtypes.bfloat16)


def make_tables():
    length = SEQ * LOCUS
    points = 2 * length
    order = np.concatenate([2 * np.arange(128), 2 * np.arange(128) + 1])
    coarse = np.arange(256) + 0.5
    angle = 2.0 * np.pi * coarse[:, None] * order[None, :] / 512.0
    first = np.concatenate([np.cos(angle), -np.sin(angle)], 0)
    first_hi, first_lo = np_halves(first)
    w1 = np.concatenate([first_hi, first_hi, first_lo], 1)
    last_hi, last_lo = np_halves(first.T / length)
    w1t = np.concatenate([last_hi, last_hi, last_lo], 1)
    fine = np.arange(256)
    angle = 2.0 * np.pi * (fine[:, None] * fine[None, :] % 256) / 256.0
    cos, sin = np.cos(angle), np.sin(angle)
    mid_hi, mid_lo = np_halves(np.block([[cos, -sin], [sin, cos]]))
    w2 = np.concatenate([mid_hi, mid_hi, mid_lo], 0)
    back_hi, back_lo = np_halves(np.block([[cos, sin], [-sin, cos]]))
    w2c = np.concatenate([back_hi, back_hi, back_lo], 0)
    angle = 2.0 * np.pi * coarse[:, None] * fine[None, :] / points
    return w1, w1t, w2, w2c, np.cos(angle).astype(np.float32), -np.sin(angle).astype(np.float32)


def tile_rows(index, count):
    return pl.ds(pl.multiple_of(index * count, count), count)


def send(src, dst, send_sem, recv_sem, seq, ch):
    pltpu.make_async_remote_copy(
        src_ref=src,
        dst_ref=dst,
        send_sem=send_sem,
        recv_sem=recv_sem,
        device_id=(seq, ch),
        device_id_type=MESH,
    ).start()


def drain(ref, sem):
    pltpu.make_async_copy(ref, ref, sem).wait()


def greet(barrier, seq, ch):
    pl.semaphore_signal(barrier, inc=1, device_id=(seq, ch), device_id_type=MESH)


def fused_kernel(
    branch_hbm,
    gate_a_hbm,
    gate_b_hbm,
    upstream_hbm,
    hidden,
    readout_hbm,
    decay_hbm,
    w1_hbm,
    w1t_hbm,
    w2_hbm,
    w2c_hbm,
    twr_hbm,
    twi_hbm,
    packed,
    w1,
    w1t,
    w2,
    w2c,
    twr,
    twi,
    branch,
    gate_a,
    gate_b,
    upstream,
    readout,
    decay,
    windows,
    feat,
    stage,
    msg,
    hmsg,
    inb,
    inh,
    sbuf,
    third,
    cross,
    dcat,
    ybuf,
    zcat,
    spec,
    qbuf,
    rcat,
    obuf,
    outb,
    outh,
    got,
    goth,
    part_f,
    got_f,
    part_w,
    got_w,
    sum_w,
    got_v,
    t_sem,
    a_sem,
    f_send,
    f_recv,
    b_send,
    b_recv,
    h_send,
    h_recv,
    g_send,
    g_recv,
    c_send,
    c_recv,
    s_send,
    s_recv,
    e_send,
    e_recv,
    o_send,
    o_recv,
    k_send,
    k_recv,
    p_send,
    p_recv,
    w_send,
    w_recv,
    v_send,
    v_recv,
):
    seq = lax.axis_index("seq")
    ch = lax.axis_index("ch")
    channel = lax.div(seq, 8)
    low = lax.rem(seq, 8)
    role = lax.rem(seq, 2)
    is_owner = owner_of(channel, ch) == seq - role
    partner = seq + 1 - 2 * role
    barrier = pltpu.get_barrier_semaphore()
    mine = tile_rows(ch, WIDTH)

    def everyone(visit):
        for ahead in (2, 1, 3, 0):
            high = lax.rem(lax.div(low, 2) + ahead, 4)

            @pl.loop(0, 32)
            def _(step):
                to = lax.rem(channel + lax.div(step, 2), 16) * 8 + high * 2 + lax.rem(step, 2)
                if ahead:
                    visit(to)
                else:

                    @pl.when(to != seq)
                    def _():
                        visit(to)

    for step in range(1, CH):
        greet(barrier, seq, lax.rem(ch + step, CH))

    arguments = [
        (hidden, feat.at[mine]),
        (branch_hbm, branch),
        (gate_a_hbm, gate_a),
        (gate_b_hbm, gate_b),
        (upstream_hbm, upstream),
        (readout_hbm, readout),
        (decay_hbm, decay),
    ]
    for index, (source, target) in enumerate(arguments):
        pltpu.make_async_copy(source, target, a_sem.at[index]).start()

    tables = [
        (w1_hbm, w1),
        (w1t_hbm, w1t),
        (w2_hbm, w2),
        (w2c_hbm, w2c),
        (twr_hbm, twr),
        (twi_hbm, twi),
    ]

    @pl.when(is_owner)
    def _():
        @pl.loop(1, SEQ)
        def _(step):
            greet(barrier, lax.rem(seq + step, SEQ), ch)

        for index, (source, target) in enumerate(tables):
            pltpu.make_async_copy(source, target, t_sem.at[index]).start()

    def stage_rows(row, value):
        for part in range(4):
            stage[pl.ds(row + part, WIDTH, stride=16), :] = value[:, part * 128 : (part + 1) * 128]

    for index, (source, target) in enumerate(arguments):
        pltpu.make_async_copy(source, target, a_sem.at[index]).wait()
    stage_rows(0, branch[...].astype(F32))
    stage_rows(4, gate_a[...].astype(F32))
    stage_rows(8, gate_b[...].astype(F32))
    stage_rows(12, upstream[...].astype(F32))
    msg[...] = stage[...].astype(BF16)
    rate = decay[...]
    scale = jnp.sqrt(less_one(-2.0 * rate) / less_one(-2.0 * rate * (SEQ * LOCUS)))
    diagonal = lax.broadcasted_iota(jnp.int32, (WIDTH, WIDTH), 0) == lax.broadcasted_iota(
        jnp.int32, (WIDTH, WIDTH), 1
    )
    position = (
        seq * LOCUS + lax.broadcasted_iota(jnp.int32, (WIDTH, LOCUS), 1)
    ).astype(F32)

    def column(values, order):
        return jnp.sum(jnp.where(diagonal, values[order : order + 1], 0.0), 1, keepdims=True)

    for order in range(2):
        windows[pl.ds(order * WIDTH, WIDTH), :] = jnp.exp(
            -column(rate, order) * position
        ) * column(scale, order)

    @pl.when(is_owner)
    def _():
        pl.semaphore_wait(barrier, 2 * WIDTH - 1 + CH - 1)

    @pl.when(jnp.logical_not(is_owner))
    def _():
        pl.semaphore_wait(barrier, 2 * WIDTH + CH - 1)

    for step in range(1, CH):
        send(hidden, feat.at[mine], f_send, f_recv, seq, lax.rem(ch + step, CH))

    slot = tile_rows(seq, 16)

    @pl.loop(0, WIDTH)
    def _(step):
        to = lax.rem(channel + step, WIDTH)
        owner = owner_of(to, ch)
        piece = msg.at[tile_rows(to, 16)]

        @pl.when(owner != seq)
        def _():
            send(piece, inb.at[slot], b_send, b_recv, owner, ch)

        @pl.when(owner == seq)
        def _():
            pltpu.make_async_copy(piece, inb.at[slot], b_recv).start()

    drain(feat.at[pl.ds(0, 3 * WIDTH)], f_recv)
    weight = readout[...]
    high, rest = halves(weight)
    middle, last = halves(weight - high.astype(F32))
    triple = jnp.dot(
        jnp.concatenate([high, middle, last], 0), feat[...], preferred_element_type=F32
    )
    filt = (triple[:32] + triple[32:64] + triple[64:]) * windows[...]
    for order in range(2):
        for part in range(4):
            hmsg[pl.ds(order * 64 + part, WIDTH, stride=4), :] = filt[
                order * WIDTH : (order + 1) * WIDTH, part * 128 : (part + 1) * 128
            ]

    @pl.loop(0, WIDTH)
    def _(step):
        to = lax.rem(channel + step, WIDTH)
        for core in range(2):
            owner = owner_of(to, ch) + core
            piece = hmsg.at[tile_rows(core * WIDTH + to, 4)]

            @pl.when(owner != seq)
            def _():
                send(piece, inh.at[tile_rows(seq, 4)], h_send, h_recv, owner, ch)

            @pl.when(owner == seq)
            def _():
                pltpu.make_async_copy(piece, inh.at[tile_rows(seq, 4)], h_recv).start()

    def chunks(body):
        @pl.loop(0, 8)
        def _(step):
            body(pl.ds(pl.multiple_of(step * 32, 32), 32), step)

    def after(base, step):
        return pl.ds(pl.multiple_of(base + step * 32, 32), 32)

    def put_rows(place, base, value):
        high, low = halves(value)
        zcat[place, pl.ds(base, 256)] = high
        zcat[place, pl.ds(base + 512, 256)] = low
        zcat[place, pl.ds(base + 1024, 256)] = high

    def forward(count, slot, start=0, after_half=None):
        width = 256 * count
        taken = pl.ds(256 * start, width)
        ybuf[:, pl.ds(0, width)] = jnp.dot(w1[...], dcat[:, taken], preferred_element_type=F32)
        for index in range(count):
            columns = pl.ds(index * 256, 256)

            def body(rows, step):
                re, im = ybuf[rows, columns], ybuf[after(256, step), columns]
                cr, ci = twr[rows, :], twi[rows, :]
                place = after(index * 256, step)
                put_rows(place, 0, re * cr - im * ci)
                put_rows(place, 256, re * ci + im * cr)

            chunks(body)
        if after_half is None:
            spec[pl.ds(slot * 256, width), :] = jnp.dot(
                zcat[pl.ds(0, width), :], w2[...], preferred_element_type=F32
            )
        else:
            for half in range(2):
                spec[pl.ds(slot * 256 + 128 * half, 128), :] = jnp.dot(
                    zcat[pl.ds(128 * half, 128), :], w2[...], preferred_element_type=F32
                )
                after_half(half)

    def inverse(pairs, start=0):
        count = len(pairs)
        width = 256 * count
        for index, (left, right, sign, flip) in enumerate(pairs):

            def body(rows, step):
                a, b = after(left * 256, step), after(right * 256, step)
                ar, ai = spec[a, pl.ds(0, 256)], spec[a, pl.ds(256, 256)]
                br, bi = spec[b, pl.ds(0, 256)], spec[b, pl.ds(256, 256)] * sign
                place = after(index * 256, step)
                put_rows(place, 0, ar * br - ai * bi)
                put_rows(place, 256, (ar * bi + ai * br) * flip)

            chunks(body)
        qbuf[pl.ds(0, width), :] = jnp.dot(
            zcat[pl.ds(0, width), :], w2c[...], preferred_element_type=F32
        )
        for index in range(count):
            columns = pl.ds(index * 256, 256)

            def body(rows, step):
                place = after(index * 256, step)
                re, im = qbuf[place, pl.ds(0, 256)], qbuf[place, pl.ds(256, 256)]
                cr, ci = twr[rows, :], twi[rows, :]
                for base, value in ((0, re * cr + im * ci), (256, im * cr - re * ci)):
                    high, low = halves(value)
                    rcat[after(base, step), columns] = high
                    rcat[after(base + 512, step), columns] = low
                    rcat[after(base + 1024, step), columns] = high

            chunks(body)
        obuf[:, pl.ds(256 * start, width)] = jnp.dot(
            w1t[...], rcat[:, pl.ds(0, width)], preferred_element_type=F32
        )

    def load(array, half):
        return jnp.concatenate(
            [sbuf[pl.ds(array * 4 + 2 * half + part, SEQ, stride=16), :] for part in range(2)], 1
        )

    def store(array, half, value):
        for part in range(2):
            sbuf[pl.ds(array * 4 + 2 * half + part, SEQ, stride=16), :] = value[
                :, part * 128 : (part + 1) * 128
            ]

    def place(half, index, high, low):
        columns = pl.ds(index * 256, 256)
        dcat[pl.ds(half * 128, 128), columns] = high
        dcat[pl.ds(256 + half * 128, 128), columns] = low
        dcat[pl.ds(512 + half * 128, 128), columns] = high

    def block(half, index):
        return obuf[pl.ds(half * 128, 128), pl.ds(index * 256, 256)]

    def swap(source, target, send_sem, recv_sem):
        return pltpu.make_async_remote_copy(
            src_ref=source,
            dst_ref=target,
            send_sem=send_sem,
            recv_sem=recv_sem,
            device_id=(partner, ch),
            device_id_type=MESH,
        )

    @pl.when(is_owner)
    def _():
        for index, (source, target) in enumerate(tables):
            pltpu.make_async_copy(source, target, t_sem.at[index]).wait()
        first_core = role == 0

        @pl.when(first_core)
        def _():
            drain(inb, b_recv)
            swap(inb, inb, g_send, g_recv).start()

        @pl.when(jnp.logical_not(first_core))
        def _():
            drain(inb, g_recv)

        sign = jnp.where(first_core, 1.0, -1.0).astype(F32)
        sbuf[...] = inb[...].astype(F32)
        for half in range(2):
            value = jnp.where(first_core, load(0, half), load(2, half) * load(3, half))
            place(half, 0, *halves(value))
        forward(1, 0)
        drain(inh, h_recv)
        for half in range(2):
            value = jnp.concatenate(
                [inh[pl.ds(2 * half + part, SEQ, stride=4), :] for part in range(2)], 1
            )
            place(half, 1, *halves(value))
        forward(1, 1, 1)
        inverse(((0, 1, sign, 1.0),))

        for half in range(2):
            rows = pl.ds(half * 128, 128)
            value = block(half, 0)
            place(half, 0, *halves(load(1, half) * value))

            @pl.when(first_core)
            def _():
                store(3, half, value)

            @pl.when(jnp.logical_not(first_core))
            def _():
                cross[rows, :] = value

        def hand_over(half, start=True):
            rows, theirs = pl.ds(512 + 128 * half, 128), pl.ds(768 + 128 * half, 128)
            copy = swap(spec.at[rows], spec.at[theirs], s_send.at[half], s_recv.at[half])
            if start:
                copy.start()
            return copy

        @pl.when(jnp.logical_not(first_core))
        def _():
            swap(cross, cross, c_send, c_recv).start()

        forward(1, 2, 0, hand_over)
        for half in range(2):
            hand_over(half, False).wait()
        inverse(((3, 0, -1.0, sign),), 1)

        for half in range(2):
            value = block(half, 1)
            for part in range(2):
                outh[pl.ds(2 * half + part, SEQ, stride=4), :] = value[
                    :, part * 128 : (part + 1) * 128
                ]
        home = role * WIDTH + channel

        @pl.loop(1, SEQ)
        def _(step):
            to = lax.rem(seq + step, SEQ)
            send(outh.at[tile_rows(to, 4)], goth.at[tile_rows(home, 4)], o_send, o_recv, to, ch)

        pltpu.make_async_copy(
            outh.at[tile_rows(seq, 4)], goth.at[tile_rows(home, 4)], o_recv
        ).start()
        inverse(((3, 1, -sign, 1.0),))

        @pl.when(jnp.logical_not(first_core))
        def _():
            for half in range(2):
                third[pl.ds(half * 128, 128), :] = block(half, 0) * load(3, half)
            swap(third, third, e_send, e_recv).start()

        @pl.when(first_core)
        def _():
            drain(cross, c_recv)
            for half in range(2):
                rows = pl.ds(half * 128, 128)
                store(0, half, block(half, 0))
                store(1, half, load(3, half) * cross[rows, :])
            drain(third, e_recv)
            for half in range(2):
                store(2, half, third[pl.ds(half * 128, 128), :])
            outb[...] = sbuf[...].astype(BF16)

            @pl.loop(1, SEQ)
            def _(step):
                to = lax.rem(seq + step, SEQ)
                send(
                    outb.at[tile_rows(to, 16)], got.at[tile_rows(channel, 16)], k_send, k_recv, to, ch
                )

            pltpu.make_async_copy(outb.at[slot], got.at[tile_rows(channel, 16)], k_recv).start()

    drain(goth, o_recv)
    grads = jnp.concatenate(
        [
            jnp.concatenate(
                [goth[pl.ds(order * 64 + part, WIDTH, stride=4), :] for part in range(4)], 1
            )
            for order in range(2)
        ],
        0,
    )
    dhw = grads * windows[...] * (1.0 / math.sqrt(SEQ * LOCUS))
    dhi, dlo = halves(dhw)
    double = lax.dot_general(
        jnp.concatenate([dhi, dlo], 0),
        feat[...],
        (((1,), (1,)), ((), ())),
        preferred_element_type=F32,
    )
    total = double[:32] + double[32:]
    part_w[...] = jnp.concatenate([total[:WIDTH], total[WIDTH:]], 1)

    @pl.loop(1, 16)
    def _(step):
        to = lax.rem(channel + step, 16) * 8 + low
        send(part_w, got_w.at[tile_rows(channel, 16)], w_send, w_recv, to, ch)

    whi, wlo = high, middle
    part_f[...] = lax.dot_general(
        jnp.concatenate([whi, whi, wlo], 0),
        jnp.concatenate([dhi, dlo, dhi], 0),
        (((0,), (0,)), ((), ())),
        preferred_element_type=F32,
    )
    for step in range(1, CH):
        to = lax.rem(ch + step, CH)
        send(part_f.at[tile_rows(to, WIDTH)], got_f.at[mine], p_send, p_recv, seq, to)
    got_w[tile_rows(channel, 16), :] = part_w[...]
    got_f[mine, :] = part_f[mine, :]
    drain(got_w.at[pl.ds(0, 15 * 16)], w_recv)
    total = got_w[pl.ds(0, 16), :]
    for index in range(1, 16):
        total = total + got_w[pl.ds(16 * index, 16), :]
    sum_w[...] = total

    @pl.loop(1, 8)
    def _(step):
        to = channel * 8 + lax.rem(low + step, 8)
        send(sum_w, got_v.at[tile_rows(low, 16)], v_send, v_recv, to, ch)

    got_v[tile_rows(low, 16), :] = total
    drain(got_f.at[pl.ds(0, 3 * WIDTH)], p_recv)
    summed = got_f[pl.ds(0, WIDTH), :]
    for index in range(1, CH):
        summed = summed + got_f[pl.ds(WIDTH * index, WIDTH), :]
    packed[pl.ds(48, WIDTH), :] = summed.astype(BF16)
    drain(got, k_recv)
    stage[...] = got[...].astype(F32)
    for index in range(3):
        packed[pl.ds(16 * index, WIDTH), :] = jnp.concatenate(
            [stage[pl.ds(4 * index + part, WIDTH, stride=16), :] for part in range(4)], 1
        ).astype(BF16)
    drain(feat.at[pl.ds(0, 3 * WIDTH)], f_send)
    drain(got_f.at[pl.ds(0, 3 * WIDTH)], p_send)
    drain(got_w.at[pl.ds(0, 15 * 16)], w_send)

    @pl.when(is_owner)
    def _():
        drain(hmsg.at[pl.ds(0, (2 * WIDTH - 1) * 4)], h_send)
        drain(outh.at[pl.ds(0, (SEQ - 1) * 4)], o_send)

        @pl.when(role == 0)
        def _():
            drain(msg.at[pl.ds(0, (WIDTH - 1) * 16)], b_send)
            drain(inb, g_send)
            drain(outb.at[pl.ds(0, (SEQ - 1) * 16)], k_send)

        @pl.when(role == 1)
        def _():
            drain(msg, b_send)
            drain(cross, c_send)
            drain(third, e_send)

    @pl.when(jnp.logical_not(is_owner))
    def _():
        drain(msg, b_send)
        drain(hmsg, h_send)

    drain(got_v.at[pl.ds(0, 7 * 16)], v_recv)
    total = got_v[pl.ds(0, 16), :]
    for index in range(1, 8):
        total = total + got_v[pl.ds(16 * index, 16), :]
    packed[pl.ds(64, 2 * WIDTH), pl.ds(0, 64)] = jnp.concatenate([total[:, :64], total[:, 64:]], 0).astype(BF16)
    drain(got_v.at[pl.ds(0, 7 * 16)], v_send)


def vmem(count):
    return [pl.BlockSpec(memory_space=pltpu.VMEM)] * count


def shape(dims, dtype):
    return jax.ShapeDtypeStruct(dims, dtype)


def body(
    signal_branch,
    leading_multiplier,
    trailing_multiplier,
    loss_upstream_adjoint,
    kernel_net_hidden,
    kernel_readout_matrix,
    kernel_attenuation,
):
    dma = pltpu.SemaphoreType.DMA
    readout = kernel_readout_matrix.reshape(2 * WIDTH, CH * WIDTH)
    tables = [jnp.asarray(table) for table in make_tables()]
    packed = pl.pallas_call(
        fused_kernel,
        out_shape=shape((96, LOCUS), BF16),
        in_specs=[pl.BlockSpec(memory_space=pltpu.HBM)] * 13,
        out_specs=vmem(1)[0],
        scratch_shapes=[pltpu.VMEM(table.shape, table.dtype) for table in tables]
        + [pltpu.VMEM((WIDTH, LOCUS), BF16)] * 4
        + [
            pltpu.VMEM((2 * WIDTH, 64), F32),
            pltpu.VMEM((2, WIDTH), F32),
            pltpu.VMEM((2 * WIDTH, LOCUS), F32),
            pltpu.VMEM((64, LOCUS), BF16),
            pltpu.VMEM((256, 128), F32),
            pltpu.VMEM((256, 128), BF16),
            pltpu.VMEM((128, 128), F32),
            pltpu.VMEM((2048, 128), BF16),
            pltpu.VMEM((512, 128), F32),
            pltpu.VMEM((2048, 128), F32),
            pltpu.VMEM((256, 256), F32),
            pltpu.VMEM((256, 256), F32),
            pltpu.VMEM((768, 512), BF16),
            pltpu.VMEM((512, 512), F32),
            pltpu.VMEM((512, 1536), BF16),
            pltpu.VMEM((1024, 512), F32),
            pltpu.VMEM((512, 512), F32),
            pltpu.VMEM((1536, 512), BF16),
            pltpu.VMEM((256, 512), F32),
            pltpu.VMEM((2048, 128), BF16),
            pltpu.VMEM((512, 128), F32),
            pltpu.VMEM((256, 128), BF16),
            pltpu.VMEM((128, 128), F32),
            pltpu.VMEM((64, LOCUS), F32),
            pltpu.VMEM((64, LOCUS), F32),
            pltpu.VMEM((16, 128), F32),
            pltpu.VMEM((256, 128), F32),
            pltpu.VMEM((16, 128), F32),
            pltpu.VMEM((128, 128), F32),
            pltpu.SemaphoreType.DMA((6,)),
            pltpu.SemaphoreType.DMA((7,)),
        ]
        + [dma] * 10
        + [pltpu.SemaphoreType.DMA((2,))] * 2
        + [dma] * 12,
        compiler_params=pltpu.CompilerParams(
            collective_id=1, has_side_effects=True, vmem_limit_bytes=VMEM_BYTES
        ),
    )(
        signal_branch,
        leading_multiplier,
        trailing_multiplier,
        loss_upstream_adjoint,
        kernel_net_hidden,
        readout,
        kernel_attenuation,
        *tables,
    )
    return (
        packed[:16],
        packed[16:32],
        packed[32:48],
        packed[64:, :64].reshape(2, WIDTH, 64),
        packed[48:64],
    )


def solution(mesh):
    in_specs = (
        P("ch", "seq"),
        P("ch", "seq"),
        P("ch", "seq"),
        P("ch", "seq"),
        P("ch", "seq"),
        P(None, "ch", None),
        P(None, "ch"),
    )
    out_specs = (
        P("ch", "seq"),
        P("ch", "seq"),
        P("ch", "seq"),
        P(None, "ch", None),
        P("ch", "seq"),
    )
    return jax.shard_map(body, mesh=mesh, in_specs=in_specs, out_specs=out_specs, check_vma=False)
```

```python
import math

import jax
import jax.numpy as jnp
import ml_dtypes
import numpy as np
from jax import lax
from jax.experimental import pallas as pl
from jax.experimental.pallas import tpu as pltpu
from jax.sharding import PartitionSpec as P

F32 = jnp.float32
BF16 = jnp.bfloat16
SEQ = 128
CH = 4
WIDTH = 16
LOCUS = 512
VMEM_BYTES = 60 * 2**20
MESH = pl.DeviceIdType.MESH


def owner_of(channel, group):
    high = lax.rem(lax.div(channel, 4) + lax.rem(channel, 4) + group, 4)
    return channel * 8 + 2 * high


def less_one(value):
    near = jnp.ones_like(value)
    for term in range(11, 1, -1):
        near = 1.0 + near * value * (1.0 / term)
    return jnp.where(jnp.abs(value) < 0.5, near * value, jnp.exp(value) - 1.0)


def halves(value):
    high = value.astype(BF16)
    return high, (value - high.astype(F32)).astype(BF16)


def np_halves(value):
    value = value.astype(np.float32)
    high = value.astype(ml_dtypes.bfloat16)
    return high, (value - high.astype(np.float32)).astype(ml_dtypes.bfloat16)


def make_tables():
    length = SEQ * LOCUS
    points = 2 * length
    order = np.concatenate([2 * np.arange(128), 2 * np.arange(128) + 1])
    coarse = np.arange(256) + 0.5
    angle = 2.0 * np.pi * coarse[:, None] * order[None, :] / 512.0
    first = np.concatenate([np.cos(angle), -np.sin(angle)], 0)
    first_hi, first_lo = np_halves(first)
    w1 = np.concatenate([first_hi, first_hi, first_lo], 1)
    last_hi, last_lo = np_halves(first.T / length)
    w1t = np.concatenate([last_hi, last_hi, last_lo], 1)
    fine = np.arange(256)
    angle = 2.0 * np.pi * (fine[:, None] * fine[None, :] % 256) / 256.0
    cos, sin = np.cos(angle), np.sin(angle)
    mid_hi, mid_lo = np_halves(np.block([[cos, -sin], [sin, cos]]))
    w2 = np.concatenate([mid_hi, mid_hi, mid_lo], 0)
    back_hi, back_lo = np_halves(np.block([[cos, sin], [-sin, cos]]))
    w2c = np.concatenate([back_hi, back_hi, back_lo], 0)
    angle = 2.0 * np.pi * coarse[:, None] * fine[None, :] / points
    return w1, w1t, w2, w2c, np.cos(angle).astype(np.float32), -np.sin(angle).astype(np.float32)


def tile_rows(index, count):
    return pl.ds(pl.multiple_of(index * count, count), count)


def send(src, dst, send_sem, recv_sem, seq, ch):
    pltpu.make_async_remote_copy(
        src_ref=src,
        dst_ref=dst,
        send_sem=send_sem,
        recv_sem=recv_sem,
        device_id=(seq, ch),
        device_id_type=MESH,
    ).start()


def drain(ref, sem):
    pltpu.make_async_copy(ref, ref, sem).wait()


def greet(barrier, seq, ch):
    pl.semaphore_signal(barrier, inc=1, device_id=(seq, ch), device_id_type=MESH)


def fused_kernel(
    branch_hbm,
    gate_a_hbm,
    gate_b_hbm,
    upstream_hbm,
    hidden,
    readout_hbm,
    decay_hbm,
    w1_hbm,
    w1t_hbm,
    w2_hbm,
    w2c_hbm,
    twr_hbm,
    twi_hbm,
    packed,
    sums,
    w1,
    w1t,
    w2,
    w2c,
    twr,
    twi,
    branch,
    gate_a,
    gate_b,
    upstream,
    readout,
    decay,
    windows,
    feat,
    stage,
    msg,
    hmsg,
    inb,
    inh,
    sbuf,
    third,
    cross,
    dcat,
    ybuf,
    zcat,
    spec,
    qbuf,
    rcat,
    obuf,
    outb,
    outh,
    got,
    goth,
    part_f,
    got_f,
    part_w,
    got_w,
    sum_w,
    got_v,
    t_sem,
    a_sem,
    f_send,
    f_recv,
    b_send,
    b_recv,
    h_send,
    h_recv,
    g_send,
    g_recv,
    c_send,
    c_recv,
    s_send,
    s_recv,
    e_send,
    e_recv,
    o_send,
    o_recv,
    k_send,
    k_recv,
    p_send,
    p_recv,
    w_send,
    w_recv,
    v_send,
    v_recv,
):
    seq = lax.axis_index("seq")
    ch = lax.axis_index("ch")
    channel = lax.div(seq, 8)
    low = lax.rem(seq, 8)
    role = lax.rem(seq, 2)
    over = lax.rem(ch + 2, CH)
    is_owner = owner_of(channel, over) == seq - role
    partner = seq + 1 - 2 * role
    barrier = pltpu.get_barrier_semaphore()
    mine = tile_rows(ch, WIDTH)

    for step in range(1, CH):
        greet(barrier, seq, lax.rem(ch + step, CH))

    arguments = [
        (hidden, feat.at[mine]),
        (branch_hbm, branch),
        (gate_a_hbm, gate_a),
        (gate_b_hbm, gate_b),
        (upstream_hbm, upstream),
        (readout_hbm, readout),
        (decay_hbm, decay),
    ]
    for index, (source, target) in enumerate(arguments):
        pltpu.make_async_copy(source, target, a_sem.at[index]).start()

    tables = [
        (w1_hbm, w1),
        (w1t_hbm, w1t),
        (w2_hbm, w2),
        (w2c_hbm, w2c),
        (twr_hbm, twr),
        (twi_hbm, twi),
    ]

    @pl.when(is_owner)
    def _():
        @pl.loop(0, SEQ)
        def _(step):
            greet(barrier, lax.rem(seq + step, SEQ), over)

        for index, (source, target) in enumerate(tables):
            pltpu.make_async_copy(source, target, t_sem.at[index]).start()

    def stage_rows(row, value):
        for part in range(4):
            stage[pl.ds(row + part, WIDTH, stride=16), :] = value[:, part * 128 : (part + 1) * 128]

    for index, (source, target) in enumerate(arguments):
        pltpu.make_async_copy(source, target, a_sem.at[index]).wait()
    stage_rows(0, branch[...].astype(F32))
    stage_rows(4, gate_a[...].astype(F32))
    stage_rows(8, gate_b[...].astype(F32))
    stage_rows(12, upstream[...].astype(F32))
    msg[...] = stage[...].astype(BF16)
    rate = decay[...]
    scale = jnp.sqrt(less_one(-2.0 * rate) / less_one(-2.0 * rate * (SEQ * LOCUS)))
    diagonal = lax.broadcasted_iota(jnp.int32, (WIDTH, WIDTH), 0) == lax.broadcasted_iota(
        jnp.int32, (WIDTH, WIDTH), 1
    )
    position = (
        seq * LOCUS + lax.broadcasted_iota(jnp.int32, (WIDTH, LOCUS), 1)
    ).astype(F32)

    def column(values, order):
        return jnp.sum(jnp.where(diagonal, values[order : order + 1], 0.0), 1, keepdims=True)

    for order in range(2):
        windows[pl.ds(order * WIDTH, WIDTH), :] = jnp.exp(
            -column(rate, order) * position
        ) * column(scale, order)

    pl.semaphore_wait(barrier, 2 * WIDTH + CH - 1)

    for step in range(1, CH):
        send(hidden, feat.at[mine], f_send, f_recv, seq, lax.rem(ch + step, CH))

    slot = tile_rows(seq, 16)

    @pl.loop(0, WIDTH)
    def _(step):
        to = lax.rem(channel + step, WIDTH)
        piece = msg.at[tile_rows(to, 16)]
        send(piece, inb.at[slot], b_send, b_recv, owner_of(to, ch), over)

    drain(feat.at[pl.ds(0, 3 * WIDTH)], f_recv)
    weight = readout[...]
    high, rest = halves(weight)
    middle, last = halves(weight - high.astype(F32))
    triple = jnp.dot(
        jnp.concatenate([high, middle, last], 0), feat[...], preferred_element_type=F32
    )
    filt = (triple[:32] + triple[32:64] + triple[64:]) * windows[...]
    for order in range(2):
        for part in range(4):
            hmsg[pl.ds(order * 64 + part, WIDTH, stride=4), :] = filt[
                order * WIDTH : (order + 1) * WIDTH, part * 128 : (part + 1) * 128
            ]

    @pl.loop(0, WIDTH)
    def _(step):
        to = lax.rem(channel + step, WIDTH)
        for core in range(2):
            piece = hmsg.at[tile_rows(core * WIDTH + to, 4)]
            owner = owner_of(to, ch) + core
            send(piece, inh.at[tile_rows(seq, 4)], h_send, h_recv, owner, over)

    def chunks(body):
        @pl.loop(0, 8)
        def _(step):
            body(pl.ds(pl.multiple_of(step * 32, 32), 32), step)

    def after(base, step):
        return pl.ds(pl.multiple_of(base + step * 32, 32), 32)

    def put_rows(place, base, value):
        high, low = halves(value)
        zcat[place, pl.ds(base, 256)] = high
        zcat[place, pl.ds(base + 512, 256)] = low
        zcat[place, pl.ds(base + 1024, 256)] = high

    def forward(count, slot, start=0, after_half=None):
        width = 256 * count
        taken = pl.ds(256 * start, width)
        ybuf[:, pl.ds(0, width)] = jnp.dot(w1[...], dcat[:, taken], preferred_element_type=F32)
        for index in range(count):
            columns = pl.ds(index * 256, 256)

            def body(rows, step):
                re, im = ybuf[rows, columns], ybuf[after(256, step), columns]
                cr, ci = twr[rows, :], twi[rows, :]
                place = after(index * 256, step)
                put_rows(place, 0, re * cr - im * ci)
                put_rows(place, 256, re * ci + im * cr)

            chunks(body)
        if after_half is None:
            spec[pl.ds(slot * 256, width), :] = jnp.dot(
                zcat[pl.ds(0, width), :], w2[...], preferred_element_type=F32
            )
        else:
            for half in range(2):
                spec[pl.ds(slot * 256 + 128 * half, 128), :] = jnp.dot(
                    zcat[pl.ds(128 * half, 128), :], w2[...], preferred_element_type=F32
                )
                after_half(half)

    def inverse(pairs, start=0):
        count = len(pairs)
        width = 256 * count
        for index, (left, right, sign, flip) in enumerate(pairs):

            def body(rows, step):
                a, b = after(left * 256, step), after(right * 256, step)
                ar, ai = spec[a, pl.ds(0, 256)], spec[a, pl.ds(256, 256)]
                br, bi = spec[b, pl.ds(0, 256)], spec[b, pl.ds(256, 256)] * sign
                place = after(index * 256, step)
                put_rows(place, 0, ar * br - ai * bi)
                put_rows(place, 256, (ar * bi + ai * br) * flip)

            chunks(body)
        qbuf[pl.ds(0, width), :] = jnp.dot(
            zcat[pl.ds(0, width), :], w2c[...], preferred_element_type=F32
        )
        for index in range(count):
            columns = pl.ds(index * 256, 256)

            def body(rows, step):
                place = after(index * 256, step)
                re, im = qbuf[place, pl.ds(0, 256)], qbuf[place, pl.ds(256, 256)]
                cr, ci = twr[rows, :], twi[rows, :]
                for base, value in ((0, re * cr + im * ci), (256, im * cr - re * ci)):
                    high, low = halves(value)
                    rcat[after(base, step), columns] = high
                    rcat[after(base + 512, step), columns] = low
                    rcat[after(base + 1024, step), columns] = high

            chunks(body)
        obuf[:, pl.ds(256 * start, width)] = jnp.dot(
            w1t[...], rcat[:, pl.ds(0, width)], preferred_element_type=F32
        )

    def load(array, half):
        return jnp.concatenate(
            [sbuf[pl.ds(array * 4 + 2 * half + part, SEQ, stride=16), :] for part in range(2)], 1
        )

    def store(array, half, value):
        for part in range(2):
            sbuf[pl.ds(array * 4 + 2 * half + part, SEQ, stride=16), :] = value[
                :, part * 128 : (part + 1) * 128
            ]

    def place(half, index, high, low):
        columns = pl.ds(index * 256, 256)
        dcat[pl.ds(half * 128, 128), columns] = high
        dcat[pl.ds(256 + half * 128, 128), columns] = low
        dcat[pl.ds(512 + half * 128, 128), columns] = high

    def block(half, index):
        return obuf[pl.ds(half * 128, 128), pl.ds(index * 256, 256)]

    def swap(source, target, send_sem, recv_sem):
        return pltpu.make_async_remote_copy(
            src_ref=source,
            dst_ref=target,
            send_sem=send_sem,
            recv_sem=recv_sem,
            device_id=(partner, ch),
            device_id_type=MESH,
        )

    @pl.when(is_owner)
    def _():
        for index, (source, target) in enumerate(tables):
            pltpu.make_async_copy(source, target, t_sem.at[index]).wait()
        first_core = role == 0

        @pl.when(first_core)
        def _():
            drain(inb, b_recv)
            swap(inb, inb, g_send, g_recv).start()

        @pl.when(jnp.logical_not(first_core))
        def _():
            drain(inb, g_recv)

        sign = jnp.where(first_core, 1.0, -1.0).astype(F32)
        sbuf[...] = inb[...].astype(F32)
        for half in range(2):
            value = jnp.where(first_core, load(0, half), load(2, half) * load(3, half))
            place(half, 0, *halves(value))
        forward(1, 0)
        drain(inh, h_recv)
        for half in range(2):
            value = jnp.concatenate(
                [inh[pl.ds(2 * half + part, SEQ, stride=4), :] for part in range(2)], 1
            )
            place(half, 1, *halves(value))
        forward(1, 1, 1)
        inverse(((0, 1, sign, 1.0),))

        for half in range(2):
            rows = pl.ds(half * 128, 128)
            value = block(half, 0)
            place(half, 0, *halves(load(1, half) * value))

            @pl.when(first_core)
            def _():
                store(3, half, value)

            @pl.when(jnp.logical_not(first_core))
            def _():
                cross[rows, :] = value

        def hand_over(half, start=True):
            rows, theirs = pl.ds(512 + 128 * half, 128), pl.ds(768 + 128 * half, 128)
            copy = swap(spec.at[rows], spec.at[theirs], s_send.at[half], s_recv.at[half])
            if start:
                copy.start()
            return copy

        @pl.when(jnp.logical_not(first_core))
        def _():
            swap(cross, cross, c_send, c_recv).start()

        forward(1, 2, 0, hand_over)
        for half in range(2):
            hand_over(half, False).wait()
        inverse(((3, 0, -1.0, sign),), 1)

        for half in range(2):
            value = block(half, 1)
            for part in range(2):
                outh[pl.ds(2 * half + part, SEQ, stride=4), :] = value[
                    :, part * 128 : (part + 1) * 128
                ]
        home = role * WIDTH + channel

        @pl.loop(0, SEQ)
        def _(step):
            to = lax.rem(seq + step, SEQ)
            send(outh.at[tile_rows(to, 4)], goth.at[tile_rows(home, 4)], o_send, o_recv, to, over)

        inverse(((3, 1, -sign, 1.0),))

        @pl.when(jnp.logical_not(first_core))
        def _():
            for half in range(2):
                third[pl.ds(half * 128, 128), :] = block(half, 0) * load(3, half)
            swap(third, third, e_send, e_recv).start()

        @pl.when(first_core)
        def _():
            drain(cross, c_recv)
            for half in range(2):
                rows = pl.ds(half * 128, 128)
                store(0, half, block(half, 0))
                store(1, half, load(3, half) * cross[rows, :])
            drain(third, e_recv)
            for half in range(2):
                store(2, half, third[pl.ds(half * 128, 128), :])
            outb[...] = sbuf[...].astype(BF16)

            target = got.at[tile_rows(channel, 16)]

            @pl.loop(0, SEQ)
            def _(step):
                to = lax.rem(seq + step, SEQ)
                send(outb.at[tile_rows(to, 16)], target, k_send, k_recv, to, over)

    drain(goth, o_recv)
    grads = jnp.concatenate(
        [
            jnp.concatenate(
                [goth[pl.ds(order * 64 + part, WIDTH, stride=4), :] for part in range(4)], 1
            )
            for order in range(2)
        ],
        0,
    )
    dhw = grads * windows[...] * (1.0 / math.sqrt(SEQ * LOCUS))
    dhi, dlo = halves(dhw)
    double = lax.dot_general(
        jnp.concatenate([dhi, dlo], 0),
        feat[...],
        (((1,), (1,)), ((), ())),
        preferred_element_type=F32,
    )
    total = double[:32] + double[32:]
    part_w[...] = jnp.concatenate([total[:WIDTH], total[WIDTH:]], 1)

    @pl.loop(1, 16)
    def _(step):
        to = lax.rem(channel + step, 16) * 8 + low
        send(part_w, got_w.at[tile_rows(channel, 16)], w_send, w_recv, to, ch)

    whi, wlo = high, middle
    part_f[...] = lax.dot_general(
        jnp.concatenate([whi, whi, wlo], 0),
        jnp.concatenate([dhi, dlo, dhi], 0),
        (((0,), (0,)), ((), ())),
        preferred_element_type=F32,
    )
    for step in range(1, CH):
        to = lax.rem(ch + step, CH)
        send(part_f.at[tile_rows(to, WIDTH)], got_f.at[mine], p_send, p_recv, seq, to)
    got_w[tile_rows(channel, 16), :] = part_w[...]
    got_f[mine, :] = part_f[mine, :]
    drain(got_w.at[pl.ds(0, 15 * 16)], w_recv)
    total = got_w[pl.ds(0, 16), :]
    for index in range(1, 16):
        total = total + got_w[pl.ds(16 * index, 16), :]
    sum_w[...] = total

    @pl.loop(1, 8)
    def _(step):
        to = channel * 8 + lax.rem(low + step, 8)
        send(sum_w, got_v.at[tile_rows(low, 16)], v_send, v_recv, to, ch)

    got_v[tile_rows(low, 16), :] = total
    drain(got_f.at[pl.ds(0, 3 * WIDTH)], p_recv)
    summed = got_f[pl.ds(0, WIDTH), :]
    for index in range(1, CH):
        summed = summed + got_f[pl.ds(WIDTH * index, WIDTH), :]
    packed[pl.ds(48, WIDTH), :] = summed.astype(BF16)
    drain(got, k_recv)
    stage[...] = got[...].astype(F32)
    for index in range(3):
        packed[pl.ds(16 * index, WIDTH), :] = jnp.concatenate(
            [stage[pl.ds(4 * index + part, WIDTH, stride=16), :] for part in range(4)], 1
        ).astype(BF16)
    drain(feat.at[pl.ds(0, 3 * WIDTH)], f_send)
    drain(got_f.at[pl.ds(0, 3 * WIDTH)], p_send)
    drain(got_w.at[pl.ds(0, 15 * 16)], w_send)

    @pl.when(is_owner)
    def _():
        drain(outh, o_send)

        @pl.when(role == 0)
        def _():
            drain(inb, g_send)
            drain(outb, k_send)

        @pl.when(role == 1)
        def _():
            drain(cross, c_send)
            drain(third, e_send)

    drain(msg, b_send)
    drain(hmsg, h_send)
    drain(got_v.at[pl.ds(0, 7 * 16)], v_recv)
    total = got_v[pl.ds(0, 16), :]
    for index in range(1, 8):
        total = total + got_v[pl.ds(16 * index, 16), :]
    sums[...] = jnp.concatenate([total[:, :64], total[:, 64:]], 0).astype(BF16)
    drain(got_v.at[pl.ds(0, 7 * 16)], v_send)


def vmem(count):
    return [pl.BlockSpec(memory_space=pltpu.VMEM)] * count


def shape(dims, dtype):
    return jax.ShapeDtypeStruct(dims, dtype)


def body(
    signal_branch,
    leading_multiplier,
    trailing_multiplier,
    loss_upstream_adjoint,
    kernel_net_hidden,
    kernel_readout_matrix,
    kernel_attenuation,
):
    dma = pltpu.SemaphoreType.DMA
    readout = kernel_readout_matrix.reshape(2 * WIDTH, CH * WIDTH)
    tables = [jnp.asarray(table) for table in make_tables()]
    packed, sums = pl.pallas_call(
        fused_kernel,
        out_shape=(shape((64, LOCUS), BF16), shape((2 * WIDTH, 64), BF16)),
        in_specs=[pl.BlockSpec(memory_space=pltpu.HBM)] * 13,
        out_specs=tuple(vmem(2)),
        scratch_shapes=[pltpu.VMEM(table.shape, table.dtype) for table in tables]
        + [pltpu.VMEM((WIDTH, LOCUS), BF16)] * 4
        + [
            pltpu.VMEM((2 * WIDTH, 64), F32),
            pltpu.VMEM((2, WIDTH), F32),
            pltpu.VMEM((2 * WIDTH, LOCUS), F32),
            pltpu.VMEM((64, LOCUS), BF16),
            pltpu.VMEM((256, 128), F32),
            pltpu.VMEM((256, 128), BF16),
            pltpu.VMEM((128, 128), F32),
            pltpu.VMEM((2048, 128), BF16),
            pltpu.VMEM((512, 128), F32),
            pltpu.VMEM((2048, 128), F32),
            pltpu.VMEM((256, 256), F32),
            pltpu.VMEM((256, 256), F32),
            pltpu.VMEM((768, 512), BF16),
            pltpu.VMEM((512, 512), F32),
            pltpu.VMEM((512, 1536), BF16),
            pltpu.VMEM((1024, 512), F32),
            pltpu.VMEM((512, 512), F32),
            pltpu.VMEM((1536, 512), BF16),
            pltpu.VMEM((256, 512), F32),
            pltpu.VMEM((2048, 128), BF16),
            pltpu.VMEM((512, 128), F32),
            pltpu.VMEM((256, 128), BF16),
            pltpu.VMEM((128, 128), F32),
            pltpu.VMEM((64, LOCUS), F32),
            pltpu.VMEM((64, LOCUS), F32),
            pltpu.VMEM((16, 128), F32),
            pltpu.VMEM((256, 128), F32),
            pltpu.VMEM((16, 128), F32),
            pltpu.VMEM((128, 128), F32),
            pltpu.SemaphoreType.DMA((6,)),
            pltpu.SemaphoreType.DMA((7,)),
        ]
        + [dma] * 10
        + [pltpu.SemaphoreType.DMA((2,))] * 2
        + [dma] * 12,
        compiler_params=pltpu.CompilerParams(
            collective_id=1, has_side_effects=True, vmem_limit_bytes=VMEM_BYTES
        ),
    )(
        signal_branch,
        leading_multiplier,
        trailing_multiplier,
        loss_upstream_adjoint,
        kernel_net_hidden,
        readout,
        kernel_attenuation,
        *tables,
    )
    return (
        packed[:16],
        packed[16:32],
        packed[32:48],
        sums.reshape(2, WIDTH, 64),
        packed[48:64],
    )


def solution(mesh):
    in_specs = (
        P("ch", "seq"),
        P("ch", "seq"),
        P("ch", "seq"),
        P("ch", "seq"),
        P("ch", "seq"),
        P(None, "ch", None),
        P(None, "ch"),
    )
    out_specs = (
        P("ch", "seq"),
        P("ch", "seq"),
        P("ch", "seq"),
        P(None, "ch", None),
        P("ch", "seq"),
    )
    return jax.shard_map(body, mesh=mesh, in_specs=in_specs, out_specs=out_specs, check_vma=False)
```
